256 devices in a mesh: gx: 16 (over z_hi, y), gy: 4 (over z_lo, core), gz: 4 (over x).
Axes of the slice: x: 4, y: 4, z: 8 (z_hi: 4, z_lo: 2; z = z_hi * 2 + z_lo), core: 2. Of those that a mesh axis runs over, the one named last changes fastest.
Arguments:
- material_fraction: float32 [256, 256, 1024], P('gx', ('gy', 'gz')), may hold values from 0 to 1, as said below
- voxel_markers: int32 [256, 256, 1024], P('gx', 'gy', 'gz'), may hold values from 0 to 2, as said below
- pressure_drive: float32 [256, 256, 1024], P('gx', 'gy', 'gz'), may hold values from 0.5 to 4
- warmth_supply: float32 [256, 256, 1024], P('gx', 'gy', 'gz'), may hold values from 0.5 to 4
- prior_velocity: float32 [256, 256, 1024], P('gx', 'gy', 'gz'), may hold values from 0 to 1
- prior_warmth_level: float32 [256, 256, 1024], P('gx', 'gy', 'gz'), may hold values from 0 to 2
Outputs:
- speed_next: float32 [256, 256, 1024], P('gx', 'gy', 'gz')
- temperature_next: float32 [256, 256, 1024], P('gx', 'gy', 'gz')
- objective_derivative: float32 [256, 256, 1024], P('gx', ('gy', 'gz'))
The draws below stay inside these ranges and needn't reach their ends.
Inputs may be any that keep to these rules, and one draw needn't show every extreme that they name: `voxel_markers`: 0 marks a design cell, 1 an inlet cell, 2 a wall cell. `material_fraction`: a design density for every cell.
All inputs are finite; a program needn't handle non-finite values.
Results may differ from the reference program's by a relative error of at most 0.00002.
Values sent between devices are 32-bit elements; how exact they have to be, the bound alone decides.
A program may use at most 128 MiB of HBM per device.

```python
import math
import jax
import jax.numpy as jnp
from jax import lax

SWEEPS = 2
GRID_LENGTH_X = 256
GRID_LENGTH_Y = 256
GRID_LENGTH_Z = 1024


def draw_voxel_markers(key, part):
    raw = jax.random.randint(key, (GRID_LENGTH_X, GRID_LENGTH_Y, GRID_LENGTH_Z), 0, 16)
    voxel_markers = jnp.where(raw == 0, 1, jnp.where(raw == 1, 2, 0)).astype(jnp.int32)
    voxel_markers = voxel_markers.at[0, 0, 0].set(1)
    voxel_markers = voxel_markers.at[0, 0, 1].set(2)
    return voxel_markers


def draw_material_fraction(key, part):
    block_cells = 5
    level_low = 0.1
    level_high = 0.9
    jitter = 0.06
    noise = 0.1
    key_bits, key_jitter, key_noise, key_shift = jax.random.split(key, 4)
    table_shape = (GRID_LENGTH_X // block_cells + 2, GRID_LENGTH_Y // block_cells + 2, GRID_LENGTH_Z // block_cells + 2)
    bits = jax.random.randint(key_bits, table_shape, 0, 2)
    levels = jnp.where(bits == 1, level_high, level_low).astype(jnp.float32)
    levels = levels + jax.random.uniform(key_jitter, table_shape, jnp.float32, -jitter, jitter)
    shifts = jax.random.randint(key_shift, (3,), 0, block_cells)
    first = (jnp.arange(GRID_LENGTH_X) + shifts[0]) // block_cells
    second = (jnp.arange(GRID_LENGTH_Y) + shifts[1]) // block_cells
    third = (jnp.arange(GRID_LENGTH_Z) + shifts[2]) // block_cells
    blocky = levels[first[:, None, None], second[None, :, None], third[None, None, :]]
    rough = jax.random.uniform(key_noise, (GRID_LENGTH_X, GRID_LENGTH_Y, GRID_LENGTH_Z), jnp.float32, -noise, noise)
    return jnp.clip(blocky + rough, 0.0, 1.0).astype(jnp.float32)


def level_of(rng, dims, pieces, least, high):
    gain, own = 1.0, jax.random.fold_in(rng, 6)
    for axis_at, shards_of in pieces:
        steps = jnp.exp(jax.random.uniform(jax.random.fold_in(own, axis_at), (shards_of,), jnp.float32, least / len(pieces), high / len(pieces)))
        gain = gain * jnp.repeat(steps, dims[axis_at] // shards_of).reshape([-1 if axis == axis_at else 1 for axis in range(len(dims))])
    return gain


def setup_inputs(seed: int = 0) -> dict:
    keys = jax.random.split(jax.random.key(seed), 7)
    return {
        "material_fraction": draw_material_fraction(jax.random.fold_in(keys[6], 71), 0),
        "voxel_markers": draw_voxel_markers(jax.random.fold_in(keys[6], 71), 0),
        "pressure_drive": jnp.clip(jnp.exp(math.log(4.0) - 2.0794415 * jax.random.uniform(keys[2], (GRID_LENGTH_X, GRID_LENGTH_Y, GRID_LENGTH_Z), jnp.float32) ** level_of(keys[2], (GRID_LENGTH_X, GRID_LENGTH_Y, GRID_LENGTH_Z), ((0, 16), (1, 4), (2, 4)), -0.2, 0.2)), 0.5, 4.0),
        "warmth_supply": jnp.clip(jnp.exp(math.log(4.0) - 2.0794415 * jax.random.uniform(keys[3], (GRID_LENGTH_X, GRID_LENGTH_Y, GRID_LENGTH_Z), jnp.float32) ** level_of(keys[3], (GRID_LENGTH_X, GRID_LENGTH_Y, GRID_LENGTH_Z), ((0, 16), (1, 4), (2, 4)), -0.2, 0.2)), 0.5, 4.0),
        "prior_velocity": jnp.clip(1.0 * jax.random.uniform(keys[4], (GRID_LENGTH_X, GRID_LENGTH_Y, GRID_LENGTH_Z), jnp.float32) ** level_of(keys[4], (GRID_LENGTH_X, GRID_LENGTH_Y, GRID_LENGTH_Z), ((0, 16), (1, 4), (2, 4)), -0.2, 0.2), 0.0, 1.0),
        "prior_warmth_level": jnp.clip(2.0 * jax.random.uniform(keys[5], (GRID_LENGTH_X, GRID_LENGTH_Y, GRID_LENGTH_Z), jnp.float32) ** level_of(keys[5], (GRID_LENGTH_X, GRID_LENGTH_Y, GRID_LENGTH_Z), ((0, 16), (1, 4), (2, 4)), -0.2, 0.2), 0.0, 2.0),
    }


kernel_taps = [(9.0 - abs(offset - 8)) / 81.0 for offset in range(17)]
sharpness = 4.0
midpoint = 0.5
penalty_max = 4.0
ramp_shape = 0.5
conduct_solid = 1.0
conduct_fluid = 0.2
advection = 2.0
heat_loss = 0.1


def smooth_along(padded_array, along, length):
    summed = kernel_taps[0] * lax.slice_in_dim(padded_array, 0, length, axis=along)
    for offset in range(1, 17):
        summed = summed + kernel_taps[offset] * lax.slice_in_dim(padded_array, offset, offset + length, axis=along)
    return summed


def pad_along(field, along, width):
    widths = [(0, 0), (0, 0), (0, 0)]
    widths[along] = (width, width)
    return jnp.pad(field, widths)


def smooth_whole(field):
    for along in range(3):
        field = smooth_along(pad_along(field, along, 8), along, field.shape[along])
    return field


def project(filtered):
    denom = jnp.tanh(sharpness * midpoint) + jnp.tanh(sharpness * (1.0 - midpoint))
    return (jnp.tanh(sharpness * midpoint) + jnp.tanh(sharpness * (filtered - midpoint))) / denom


def project_slope(filtered):
    denom = jnp.tanh(sharpness * midpoint) + jnp.tanh(sharpness * (1.0 - midpoint))
    hyper = jnp.tanh(sharpness * (filtered - midpoint))
    return sharpness * (1.0 - hyper * hyper) / denom


def neighbour_sum(padded_array):
    summed = padded_array[..., 2:, 1:-1, 1:-1] + padded_array[..., :-2, 1:-1, 1:-1]
    summed = summed + padded_array[..., 1:-1, 2:, 1:-1] + padded_array[..., 1:-1, :-2, 1:-1]
    return summed + padded_array[..., 1:-1, 1:-1, 2:] + padded_array[..., 1:-1, 1:-1, :-2]


def spread_warmth(padded_array, center):
    parts = [padded_array[2:, 1:-1, 1:-1], padded_array[:-2, 1:-1, 1:-1], padded_array[1:-1, 2:, 1:-1],
             padded_array[1:-1, :-2, 1:-1], padded_array[1:-1, 1:-1, 2:], padded_array[1:-1, 1:-1, :-2]]
    summed = (parts[0] - center) ** 2
    for other in parts[1:]:
        summed = summed + (other - center) ** 2
    return 0.5 * summed


def jacobi_update(padded_array, prior_velocity, temper, drag_coefficient, heat_transfer_coefficient, pressure_drive, warmth_supply, voxel_markers):
    beside_all = neighbour_sum(padded_array)
    speed_new = (pressure_drive + beside_all[0]) / (6.0 + drag_coefficient)
    upwind = padded_array[1, :-2, 1:-1, 1:-1]
    temp_new = (warmth_supply + heat_transfer_coefficient * beside_all[1] + advection * prior_velocity * upwind) / (6.0 * heat_transfer_coefficient + advection * prior_velocity + heat_loss)
    speed_new = jnp.where(voxel_markers == 1, 1.0, jnp.where(voxel_markers == 2, 0.0, speed_new))
    temp_new = jnp.where(voxel_markers == 1, 0.0, temp_new)
    return speed_new, temp_new


def padded_pile(prior_velocity, temper):
    return jnp.pad(jnp.stack([prior_velocity, temper]), ((0, 0), (1, 1), (1, 1), (1, 1)))


def reference(material_fraction, voxel_markers, pressure_drive, warmth_supply, prior_velocity, prior_warmth_level):
    filtered = smooth_whole(material_fraction)
    dens = project(filtered)
    drag_coefficient = penalty_max * ramp_shape * (1.0 - dens) / (ramp_shape + dens)
    heat_transfer_coefficient = conduct_solid + (conduct_fluid - conduct_solid) * dens
    for sweep_id in range(SWEEPS):
        padded_array = padded_pile(prior_velocity, prior_warmth_level)
        prior_velocity, prior_warmth_level = jacobi_update(padded_array, prior_velocity, prior_warmth_level, drag_coefficient, heat_transfer_coefficient, pressure_drive, warmth_supply, voxel_markers)
    padded_array = padded_pile(prior_velocity, prior_warmth_level)
    warmth_content = spread_warmth(padded_array[1], prior_warmth_level)
    penalty_slope = -penalty_max * ramp_shape * (1.0 + ramp_shape) / ((ramp_shape + dens) ** 2)
    local = penalty_slope * prior_velocity * prior_velocity + (conduct_fluid - conduct_solid) * warmth_content
    objective_derivative = smooth_whole(local * project_slope(filtered))
    return prior_velocity, prior_warmth_level, objective_derivative
```

```python
import functools
import math

import jax
import jax.numpy as jnp
from jax import lax
from jax.experimental import pallas as pl
from jax.experimental.pallas import tpu as pltpu
from jax.sharding import PartitionSpec as P

MESH = pl.DeviceIdType.MESH
F32 = jnp.float32

TANH2 = math.tanh(2.0)
SCALE = 1.0 / 81.0**3


def tri_lanes(x):
    n = x.shape[1]
    a = x + pltpu.roll(x, 1, 1)
    a = a + pltpu.roll(a, 2, 1)
    a = a + pltpu.roll(a, 4, 1)
    a = a + pltpu.roll(x, 8, 1)
    b = a + pltpu.roll(a, n - 1, 1)
    b = b + pltpu.roll(b, n - 2, 1)
    b = b + pltpu.roll(b, n - 4, 1)
    return b + pltpu.roll(a, n - 8, 1)


def tri_rows(x):
    n = x.shape[0]
    a = x + pltpu.roll(x, 1, 0)
    a = a + pltpu.roll(a, 2, 0)
    a = a + pltpu.roll(a, 4, 0)
    a = a + pltpu.roll(x, 8, 0)
    b = a + pltpu.roll(a, 1, 0)
    b = b + pltpu.roll(b, 2, 0)
    b = b + pltpu.roll(b, 4, 0)
    b = b + pltpu.roll(a, 8, 0)
    return b[16:]


def box_lead(x):
    a = x[1:] + x[:-1]
    a = a[2:] + a[:-2]
    a = a[4:] + a[:-4]
    return a[1:] + x[: x.shape[0] - 8]


def tri_lead(x):
    return box_lead(box_lead(x))


class Exchange:
    def __init__(self, axis, low, high, land_low, land_high, sems):
        self.axis, self.low_src, self.high_src = axis, low, high
        self.land_low, self.land_high, self.sems = land_low, land_high, sems
        self.at, self.count = lax.axis_index(axis), lax.axis_size(axis)

    def low(self):
        return pltpu.make_async_remote_copy(
            src_ref=self.low_src, dst_ref=self.land_high, send_sem=self.sems[0], recv_sem=self.sems[1],
            device_id={self.axis: self.at - 1}, device_id_type=MESH)

    def high(self):
        return pltpu.make_async_remote_copy(
            src_ref=self.high_src, dst_ref=self.land_low, send_sem=self.sems[2], recv_sem=self.sems[3],
            device_id={self.axis: self.at + 1}, device_id_type=MESH)

    def has_low(self):
        return self.at > 0

    def has_high(self):
        return self.at < self.count - 1

    def start(self):
        @pl.when(self.has_low())
        def _():
            self.low().start()

        @pl.when(self.has_high())
        def _():
            self.high().start()

    def wait(self):
        @pl.when(self.has_low())
        def _():
            self.high().wait_recv()

        @pl.when(self.has_high())
        def _():
            self.low().wait_recv()

    def finish(self):
        @pl.when(self.has_low())
        def _():
            self.low().wait_send()

        @pl.when(self.has_high())
        def _():
            self.high().wait_send()

    def clear(self):
        @pl.when(self.at == 0)
        def _():
            self.land_low[...] = jnp.zeros(self.land_low.shape, F32)

        @pl.when(self.at == self.count - 1)
        def _():
            self.land_high[...] = jnp.zeros(self.land_high.shape, F32)


def kernel(mat_h, mark_h, press_h, warm_h, vel_h, temp_h, speed_o, temper_o, deriv_o,
           mat, mark, press, warm, st0, st1, st2, rinv, cond, gain, slope,
           zs, yl1, yh1, ds, q1, q2, us, yl2, yh2, ws, slab, outs,
           lx_lo, lx_hi, ys, yl, zsnd, zl,
           in_sem, out_sem, y1_sem, y2_sem, g1_sem, g2_sem, a1_sem, a2_sem, x_sem, r_sem, c_sem):
    gx, gy, gz = lax.axis_index("gx"), lax.axis_index("gy"), lax.axis_index("gz")
    nx, ny, nz = lax.axis_size("gx"), lax.axis_size("gy"), lax.axis_size("gz")
    lead, rows, cols = st0.shape[1:]
    thin = rows // nz

    loads = [pltpu.make_async_copy(src, dst, in_sem.at[k]) for k, (src, dst) in enumerate(
        [(mat_h, mat), (vel_h, st0.at[0]), (temp_h, st0.at[1]), (press_h, press), (warm_h, warm), (mark_h, mark)])]
    for load in loads:
        load.start()

    barrier = pltpu.get_barrier_semaphore()
    for axis, at, count in (("gx", gx, nx), ("gy", gy, ny)):
        @pl.when(at > 0)
        def _():
            pl.semaphore_signal(barrier, inc=1, device_id={axis: at - 1}, device_id_type=MESH)

        @pl.when(at < count - 1)
        def _():
            pl.semaphore_signal(barrier, inc=1, device_id={axis: at + 1}, device_id_type=MESH)
    for hop in range(1, nz):
        pl.semaphore_signal(barrier, inc=1, device_id={"gz": lax.rem(gz + hop, nz)}, device_id_type=MESH)

    y1 = [Exchange("gx", zs.at[c, 0:8], zs.at[c, lead - 8:lead], yl1.at[c], yh1.at[c],
                   [y1_sem.at[c, k] for k in range(4)]) for c in range(nz)]
    y2 = [Exchange("gx", us.at[c, 0:8], us.at[c, lead - 8:lead], yl2.at[c], yh2.at[c],
                   [y2_sem.at[c, k] for k in range(4)]) for c in range(nz)]
    g1 = Exchange("gy", q1.at[:, 8:16], q1.at[:, rows:rows + 8], q1.at[:, 0:8], q1.at[:, rows + 8:rows + 16],
                  [g1_sem.at[k] for k in range(4)])
    g2 = Exchange("gy", q2.at[:, 8:16], q2.at[:, rows:rows + 8], q2.at[:, 0:8], q2.at[:, rows + 8:rows + 16],
                  [g2_sem.at[k] for k in range(4)])
    states = (st0, st1, st2)
    xs, rs, cs = [], [], []
    for r in range(3):
        which = slice(1, 2) if r == 2 else slice(0, 2)
        xs.append(Exchange("gx", states[r].at[which, 0], states[r].at[which, lead - 1],
                           lx_lo.at[r, which], lx_hi.at[r, which], [x_sem.at[r, k] for k in range(4)]))
        rs.append(Exchange("gy", ys.at[r, 0], ys.at[r, 1], yl.at[r, 0], yl.at[r, 1], [r_sem.at[r, k] for k in range(4)]))
        cs.append(Exchange("gz", zsnd.at[r, 0], zsnd.at[r, 1], zl.at[r, 0], zl.at[r, 1], [c_sem.at[r, k] for k in range(4)]))
    for e in y1 + y2 + [g1, g2] + xs + rs + cs:
        e.clear()

    loads[0].wait()

    def smooth_z1(i, carry):
        x = jnp.concatenate([mat[i], jnp.zeros((thin, 128), F32)], axis=1)
        x = tri_lanes(x)
        for c in range(nz):
            zs[c, i] = x[:, c * cols:(c + 1) * cols]
        return carry

    lax.fori_loop(0, lead, smooth_z1, 0)

    pl.semaphore_wait(barrier, (nz - 1) + (gx > 0).astype(jnp.int32) + (gx < nx - 1).astype(jnp.int32)
                      + (gy > 0).astype(jnp.int32) + (gy < ny - 1).astype(jnp.int32))

    def chunk_copy(src, dst, c, slot, sems):
        return pltpu.make_async_remote_copy(src_ref=src, dst_ref=dst, send_sem=sems.at[0, slot], recv_sem=sems.at[1, slot],
                                            device_id={"gz": c}, device_id_type=MESH)

    def tile_rows(g):
        return pl.ds(pl.multiple_of(8 + thin * g, 8), thin)

    def y_exchange(src, low, high, c, sems):
        return Exchange("gx", src.at[c, 0:8], src.at[c, lead - 8:lead], low.at[c], high.at[c], [sems.at[c, k] for k in range(4)])

    def order(t):
        return lax.rem(gz + 1 + t, nz)

    for t in range(nz):
        y_exchange(zs, yl1, yh1, order(t), y1_sem).start()

    loads[1].wait()
    loads[2].wait()
    xs[0].start()
    row_at = lax.broadcasted_iota(jnp.int32, (rows, cols), 0)
    lane_at = lax.broadcasted_iota(jnp.int32, (rows, cols), 1)
    lane_128 = lax.broadcasted_iota(jnp.int32, (rows, 128), 1)

    def pack(r, i, k, field, sides):
        at = k * lead + i
        ys[r, 0, pl.ds(at, 1), :] = field[0:1, :]
        ys[r, 1, pl.ds(at, 1), :] = field[rows - 1:rows, :]
        low, high = sides
        low = jnp.where(lane_128 == at, pltpu.roll(field[:, 0:128], at, 1), low)
        high = jnp.where(lane_128 == at, pltpu.roll(field[:, cols - 128:cols], at + 1, 1), high)
        return low, high

    def pack_first(i, sides):
        sides = pack(0, i, 0, st0[0, i], sides)
        return pack(0, i, 1, st0[1, i], sides)

    blank = (jnp.zeros((rows, 128), F32), jnp.zeros((rows, 128), F32))
    sides = lax.fori_loop(0, lead, pack_first, blank)
    zsnd[0, 0], zsnd[0, 1] = sides
    rs[0].start()
    cs[0].start()

    def smooth_lead(src, low, high, c, dst):
        for a in range(thin // 8):
            for b in range(cols // 128):
                part = (slice(None), slice(8 * a, 8 * a + 8), slice(128 * b, 128 * b + 128))
                x = jnp.concatenate([low[(c,) + part], src[(c,) + part], high[(c,) + part]], axis=0)
                dst(part, tri_lead(x))

    for t in range(nz):
        c = order(t)
        y_exchange(zs, yl1, yh1, c, y1_sem).wait()
        if t < nz - 1:
            def put(part, value):
                ds[(c,) + part] = value
            smooth_lead(zs, yl1, yh1, c, put)
            chunk_copy(ds.at[c], q1.at[:, tile_rows(gz), :], c, t, a1_sem).start()
        else:
            def put(part, value):
                q1[:, pl.ds(pl.multiple_of(8 + thin * gz + part[1].start, 8), 8), part[2]] = value
            smooth_lead(zs, yl1, yh1, c, put)
    for t in range(nz - 1):
        source = lax.rem(gz - 1 - t + nz, nz)
        chunk_copy(ds.at[source], q1.at[:, tile_rows(source), :], source, t, a1_sem).wait_recv()

    g1.start()
    for k in (3, 4, 5):
        loads[k].wait()
    g1.wait()

    def project(i, carry):
        x = tri_rows(q1[i]) * SCALE
        th = jnp.tanh(4.0 * (x - 0.5))
        dens = (TANH2 + th) * (0.5 / TANH2)
        slop = (1.0 - th * th) * (2.0 / TANH2)
        inv = 1.0 / (0.5 + dens)
        rinv[i] = 1.0 / (6.0 + 2.0 * (1.0 - dens) * inv)
        cond[i] = 1.0 - 0.8 * dens
        gain[i] = -3.0 * inv * inv * slop
        slope[i] = slop
        return carry

    lax.fori_loop(0, lead, project, 0)

    def beside(r, k, i, field):
        at = k * lead + i
        up = jnp.where(row_at == 0, yl[r, 0, pl.ds(at, 1), :], pltpu.roll(field, 1, 0))
        down = jnp.where(row_at == rows - 1, yl[r, 1, pl.ds(at, 1), :], pltpu.roll(field, rows - 1, 0))
        low = pltpu.roll(zl[r, 0], lax.rem(128 - at, 128), 1)
        high = pltpu.roll(zl[r, 1], 127 - at, 1)
        left, right = pltpu.roll(field, 1, 1), pltpu.roll(field, cols - 1, 1)
        left = jnp.concatenate([jnp.where(lane_128 == 0, low, left[:, 0:128]), left[:, 128:]], axis=1)
        right = jnp.concatenate([right[:, :cols - 128], jnp.where(lane_128 == 127, high, right[:, cols - 128:])], axis=1)
        return up, down, left, right

    def sweep(r, i, before, after):
        old, new = states[r], states[r + 1]
        s, t = old[0, i], old[1, i]
        upwind = before(1)
        marks = mark[i]
        a, b, c, d = beside(r, 0, i, s)
        total = before(0) + after(0) + ((a + b) + (c + d))
        fresh_s = (press[i] + total) * rinv[i]
        fresh_s = jnp.where(marks == 1, 1.0, jnp.where(marks == 2, 0.0, fresh_s))
        a, b, c, d = beside(r, 1, i, t)
        total = upwind + after(1) + ((a + b) + (c + d))
        h, drift = cond[i], 2.0 * s
        fresh_t = (warm[i] + h * total + drift * upwind) / (6.0 * h + drift + 0.1)
        fresh_t = jnp.where(marks == 1, 0.0, fresh_t)
        new[0, i], new[1, i] = fresh_s, fresh_t
        return fresh_s, fresh_t

    def run_sweep(r):
        old = states[r]

        def packed(i, sides, fresh):
            if r == 0:
                sides = pack(1, i, 0, fresh[0], sides)
            return pack(r + 1, i, 1, fresh[1], sides)

        def inner(i, sides):
            return packed(i, sides, sweep(r, i, lambda k: old[k, i - 1], lambda k: old[k, i + 1]))

        rs[r].wait()
        cs[r].wait()
        if r == 0:
            xs[r].wait()
        else:
            sides = lax.fori_loop(1, lead - 1, inner, blank)
            xs[r].wait()
        first = sweep(r, 0, lambda k: lx_lo[r, k], lambda k: old[k, 1])
        last = sweep(r, lead - 1, lambda k: old[k, lead - 2], lambda k: lx_hi[r, k])
        xs[r + 1].start()
        if r == 0:
            sides = packed(0, blank, first)
            sides = packed(lead - 1, sides, last)
            sides = lax.fori_loop(1, lead - 1, inner, sides)
        else:
            sides = packed(0, sides, first)
            sides = packed(lead - 1, sides, last)
        zsnd[r + 1, 0], zsnd[r + 1, 1] = sides
        rs[r + 1].start()
        cs[r + 1].start()

    ys[2] = jnp.zeros(ys.shape[1:], F32)
    run_sweep(0)
    run_sweep(1)
    stores = [pltpu.make_async_copy(st2.at[0], speed_o, out_sem.at[0]), pltpu.make_async_copy(st2.at[1], temper_o, out_sem.at[1])]
    for store in stores:
        store.start()

    def spread(i, before, after):
        s, t = st2[0, i], st2[1, i]
        energy = (before - t) ** 2 + (after - t) ** 2
        for other in beside(2, 1, i, t):
            energy = energy + (other - t) ** 2
        q2[i, 8:rows + 8, :] = gain[i] * s * s - 0.4 * energy * slope[i]

    rs[2].wait()
    cs[2].wait()

    def inner_spread(i, carry):
        spread(i, st2[1, i - 1], st2[1, i + 1])
        return carry

    lax.fori_loop(1, lead - 1, inner_spread, 0)
    xs[2].wait()
    spread(0, lx_lo[2, 1], st2[1, 1])
    spread(lead - 1, st2[1, lead - 2], lx_hi[2, 1])
    g2.start()
    g2.wait()

    def smooth_rows(i, carry):
        x = tri_rows(q2[i])
        for c in range(nz):
            us[c, i] = x[c * thin:(c + 1) * thin, :]
        return carry

    lax.fori_loop(0, lead, smooth_rows, 0)
    for t in range(nz):
        y_exchange(us, yl2, yh2, order(t), y2_sem).start()
    for t in range(nz):
        c = order(t)
        y_exchange(us, yl2, yh2, c, y2_sem).wait()
        if t < nz - 1:
            def put(part, value):
                ws[(c,) + part] = value
            smooth_lead(us, yl2, yh2, c, put)
            chunk_copy(ws.at[c], slab.at[gz], c, t, a2_sem).start()
        else:
            def put(part, value):
                slab[(gz,) + part] = value
            smooth_lead(us, yl2, yh2, c, put)
    for t in range(nz - 1):
        source = lax.rem(gz - 1 - t + nz, nz)
        chunk_copy(ws.at[source], slab.at[source], source, t, a2_sem).wait_recv()

    def smooth_z2(i, carry):
        x = jnp.concatenate([slab[c, i] for c in range(nz)] + [jnp.zeros((thin, 128), F32)], axis=1)
        outs[i] = tri_lanes(x)[:, :nz * cols] * SCALE
        return carry

    lax.fori_loop(0, lead, smooth_z2, 0)
    stores.append(pltpu.make_async_copy(outs, deriv_o, out_sem.at[2]))
    stores[2].start()

    for e in y1 + y2 + [g1, g2] + xs + rs + cs:
        e.finish()
    for t in range(nz - 1):
        c = order(t)
        chunk_copy(ds.at[c], q1.at[:, tile_rows(gz), :], c, t, a1_sem).wait_send()
        chunk_copy(ws.at[c], slab.at[gz], c, t, a2_sem).wait_send()
    for store in stores:
        store.wait()


def solution(mesh):
    nz = mesh.shape["gz"]

    def body(mat, mark, press, warm, vel, temp):
        lead, rows, cols = vel.shape
        thin, full = mat.shape[1:]
        tile, flat = (lead, rows, cols), (lead, thin, full)
        dma = pltpu.SemaphoreType.DMA
        vmem = lambda *shape: pltpu.VMEM(shape, F32)
        chunks, half = (nz, lead, thin, cols), (nz, 8, thin, cols)
        return pl.pallas_call(
            kernel,
            name="design_iteration",
            out_shape=[jax.ShapeDtypeStruct(tile, F32), jax.ShapeDtypeStruct(tile, F32), jax.ShapeDtypeStruct(flat, F32)],
            in_specs=[pl.BlockSpec(memory_space=pl.ANY)] * 6,
            out_specs=[pl.BlockSpec(memory_space=pl.ANY)] * 3,
            scratch_shapes=[
                vmem(*flat), pltpu.VMEM(tile, jnp.int32), vmem(*tile), vmem(*tile),
                vmem(2, *tile), vmem(2, *tile), vmem(2, *tile),
                vmem(*tile), vmem(*tile), vmem(*tile), vmem(*tile),
                vmem(*chunks), vmem(*half), vmem(*half), vmem(*chunks),
                vmem(lead, rows + 16, cols), vmem(lead, rows + 16, cols),
                vmem(*chunks), vmem(*half), vmem(*half), vmem(*chunks), vmem(*chunks), vmem(*flat),
                vmem(3, 2, rows, cols), vmem(3, 2, rows, cols),
                vmem(3, 2, 2 * lead, cols), vmem(3, 2, 2 * lead, cols),
                vmem(3, 2, rows, 128), vmem(3, 2, rows, 128),
                dma((6,)), dma((3,)), dma((nz, 4)), dma((nz, 4)), dma((4,)), dma((4,)),
                dma((2, nz)), dma((2, nz)), dma((3, 4)), dma((3, 4)), dma((3, 4)),
            ],
            compiler_params=pltpu.CompilerParams(
                collective_id=0, has_side_effects=True, vmem_limit_bytes=48 * 1024 * 1024),
        )(mat, mark, press, warm, vel, temp)

    tiles, slabs = P("gx", "gy", "gz"), P("gx", ("gy", "gz"), None)
    return jax.shard_map(body, mesh=mesh, in_specs=(slabs,) + (tiles,) * 5, out_specs=(tiles, tiles, slabs), check_vma=False)
```

```python
import functools
import math

import jax
import jax.numpy as jnp
from jax import lax
from jax.experimental import pallas as pl
from jax.experimental.pallas import tpu as pltpu
from jax.sharding import PartitionSpec as P

MESH = pl.DeviceIdType.MESH
F32 = jnp.float32

TANH2 = math.tanh(2.0)
GROUP = 4
SCALE = 1.0 / 81.0**3


def band_rows(n):
    row = lax.broadcasted_iota(jnp.int32, (n + 256, n), 0)
    col = lax.broadcasted_iota(jnp.int32, (n + 256, n), 1)
    return jnp.maximum(9 - jnp.abs(row - 128 - col), 0).astype(F32).astype(jnp.bfloat16)


def tri_lanes(x, band):
    top = x.astype(jnp.bfloat16)
    rest = x - top.astype(F32)
    mid = rest.astype(jnp.bfloat16)
    low = (rest - mid.astype(F32)).astype(jnp.bfloat16)
    y = jnp.dot(jnp.concatenate([top, mid, low], axis=0), band, preferred_element_type=F32)
    n = x.shape[0]
    return y[:n] + (y[n:2 * n] + y[2 * n:])


def tri_rows(x):
    n = x.shape[0]
    a = x + pltpu.roll(x, 1, 0)
    a = a + pltpu.roll(a, 2, 0)
    a = a + pltpu.roll(a, 4, 0)
    a = a + pltpu.roll(x, 8, 0)
    b = a + pltpu.roll(a, 1, 0)
    b = b + pltpu.roll(b, 2, 0)
    b = b + pltpu.roll(b, 4, 0)
    b = b + pltpu.roll(a, 8, 0)
    return b[16:]


def box_lead(x):
    a = x[1:] + x[:-1]
    a = a[2:] + a[:-2]
    a = a[4:] + a[:-4]
    return a[1:] + x[: x.shape[0] - 8]


def tri_lead(x):
    return box_lead(box_lead(x))


def when(condition, act):
    if condition is None:
        act()
    else:
        pl.when(condition)(act)


class Copy:
    def __init__(self, src, dst, sems, target, sends=None, receives=None, here=None):
        self.src, self.dst, self.sems, self.target = src, dst, sems, target
        self.sends, self.receives, self.here = sends, receives, dst if here is None else here

    def make(self, dst):
        return pltpu.make_async_remote_copy(src_ref=self.src, dst_ref=dst, send_sem=self.sems[0], recv_sem=self.sems[1],
                                            device_id=self.target, device_id_type=MESH)

    def start(self):
        when(self.sends, lambda: self.make(self.dst).start())

    def wait(self):
        when(self.receives, lambda: self.make(self.here).wait_recv())

    def finish(self):
        when(self.sends, lambda: self.make(self.dst).wait_send())


def kernel(mat_h, mark_h, press_h, warm_h, vel_h, temp_h, speed_o, temper_o, deriv_o,
           mat, mark, press, warm, st0, st1, st2, rinv, cond, gain, slope, band,
           zs, yl1, yh1, ds, q1, q2, us, yl2, yh2, ws, slab, outs, fy1, fy2,
           lx_lo, lx_hi, ys, yl, zsnd, zl, in_sem, out_sem, link_sem):
    gx, gy, gz = lax.axis_index("gx"), lax.axis_index("gy"), lax.axis_index("gz")
    nx, ny, nz = lax.axis_size("gx"), lax.axis_size("gy"), lax.axis_size("gz")
    lead, rows, cols = st0.shape[1:]
    thin = rows // nz
    full = nz * cols

    loads = [pltpu.make_async_copy(src, dst, in_sem.at[k]) for k, (src, dst) in enumerate(
        [(mat_h, mat), (vel_h, st0.at[0]), (temp_h, st0.at[1]), (press_h, press), (warm_h, warm), (mark_h, mark)])]
    for load in loads:
        load.start()

    edge_first, edge_last = lax.rem(gx, GROUP) == 0, lax.rem(gx, GROUP) == GROUP - 1
    at_edge = jnp.logical_or(edge_first, edge_last)
    both = jnp.logical_and
    has_before, has_after = gx >= GROUP, gx < nx - GROUP
    partners = [("gx", gx - 1, gx > 0), ("gx", gx + 1, gx < nx - 1), ("gy", gy - 1, gy > 0), ("gy", gy + 1, gy < ny - 1)]
    if nx > GROUP:
        partners += [("gx", gx - GROUP, both(at_edge, has_before)), ("gx", gx + GROUP, both(at_edge, has_after)),
                     ("gx", gx + GROUP - 1, edge_first), ("gx", gx - GROUP + 1, edge_last)]
    barrier = pltpu.get_barrier_semaphore()
    greeted = jnp.int32(nz - 1)
    for axis, to, there in partners:
        def greet():
            pl.semaphore_signal(barrier, inc=1, device_id={axis: to}, device_id_type=MESH)
        pl.when(there)(greet)
        greeted = greeted + there.astype(jnp.int32)
    for hop in range(1, nz):
        pl.semaphore_signal(barrier, inc=1, device_id={"gz": lax.rem(gz + hop, nz)}, device_id_type=MESH)

    used = [0]

    def sems():
        used[0] += 1
        return link_sem.at[0, used[0] - 1], link_sem.at[1, used[0] - 1]

    started = []

    def start(*copies):
        for copy in copies:
            copy.start()
            started.append(copy)

    def wait(*copies):
        for copy in copies:
            copy.wait()

    def finish(*copies):
        for copy in copies:
            copy.finish()
            started.remove(copy)

    def begin_lead(halos, *steps):
        for t in steps:
            near, legs_in, _ = halos[t]
            start(*legs_in, *near)

    def exchange(axis, low, high, land_low, land_high):
        at, count = lax.axis_index(axis), lax.axis_size(axis)

        @pl.when(at == 0)
        def _():
            land_low[...] = jnp.zeros(land_low.shape, F32)

        @pl.when(at == count - 1)
        def _():
            land_high[...] = jnp.zeros(land_high.shape, F32)

        return (Copy(high, land_low, sems(), {axis: at + 1}, at < count - 1, at > 0),
                Copy(low, land_high, sems(), {axis: at - 1}, at > 0, at < count - 1))

    hops = [2, 1, 3, 0] if nz == 4 else list(range(1, nz)) + [0]
    order = [lax.rem(gz + hop, nz) for hop in hops]

    def lead_halos(src, low, high, held):
        @pl.when(gx == 0)
        def _():
            low[...] = jnp.zeros(low.shape, F32)

        @pl.when(gx == nx - 1)
        def _():
            high[...] = jnp.zeros(high.shape, F32)

        h = thin // 2
        plans = []
        for t in range(nz):
            c = order[t]
            near, legs_in, legs_out = [], [], []
            for up in (True, False):
                out = src.at[c, lead - 8:lead] if up else src.at[c, 0:8]
                land = (low if up else high).at[c]
                step = 1 if up else -1
                sends, receives = (gx < nx - 1, gx > 0) if up else (gx > 0, gx < nx - 1)
                crosses = both(edge_last, sends) if up else both(edge_first, sends)
                if nx > GROUP:
                    near.append(Copy(out.at[:, 0:h], land.at[:, 0:h], sems(), {"gx": gx + step}, sends, receives))
                    pair = sems()
                    direct = both(sends, jnp.logical_not(crosses))
                    near.append(Copy(out.at[:, h:], land.at[:, h:], pair, {"gx": gx + step}, direct, receives))
                    first, second = -step * (GROUP - 1), step * GROUP
                    holds = both(edge_first, has_after) if up else both(edge_last, has_before)
                    legs_in.append(Copy(out.at[:, h:], held.at[t], sems(), {"gx": gx + first}, crosses, holds))
                    legs_out.append(Copy(held.at[t], land.at[:, h:], (sems()[0], pair[1]), {"gx": gx + second}, holds))
                else:
                    near.append(Copy(out, land, sems(), {"gx": gx + step}, sends, receives))
            plans.append((near, legs_in, legs_out))
        return plans

    def to_chunks(src, place):
        return [Copy(src.at[order[t]], place(gz), sems(), {"gz": order[t]}, here=place(lax.rem(gz + nz - hops[t], nz)))
                for t in range(nz - 1)]

    def tile_rows(g):
        return q1.at[:, pl.ds(pl.multiple_of(8 + thin * g, 8), thin), :]

    y1, y2 = lead_halos(zs, yl1, yh1, fy1), lead_halos(us, yl2, yh2, fy2)
    a1, a2 = to_chunks(ds, tile_rows), to_chunks(ws, lambda g: slab.at[g])
    g1 = exchange("gy", q1.at[:, 8:16], q1.at[:, rows:rows + 8], q1.at[:, 0:8], q1.at[:, rows + 8:rows + 16])
    g2 = exchange("gy", q2.at[:, 8:16], q2.at[:, rows:rows + 8], q2.at[:, 0:8], q2.at[:, rows + 8:rows + 16])
    states = (st0, st1, st2)
    xs, rs, cs = [], [], []
    for r in range(3):
        which = slice(1, 2) if r == 2 else slice(0, 2)
        xs.append(exchange("gx", states[r].at[which, 0], states[r].at[which, lead - 1], lx_lo.at[r, which], lx_hi.at[r, which]))
        rs.append(exchange("gy", ys.at[r, 0], ys.at[r, 1], yl.at[r, 0], yl.at[r, 1]))
        cs.append(exchange("gz", zsnd.at[r, 0], zsnd.at[r, 1], zl.at[r, 0], zl.at[r, 1]))

    def smooth_full(piece, c, m):
        first, last = max(0, c * cols - 128), min(full, (c + 1) * cols + 128)
        skip = first - (c * cols - 128)
        x = piece(pl.ds(8 * m, 8), first, last).reshape(8 * thin, last - first)
        return tri_lanes(x, band[skip:skip + last - first, :]).reshape(8, thin, cols)

    band[...] = band_rows(cols)
    loads[0].wait()

    def smooth_z1(m, carry):
        for c in range(nz):
            zs[c, pl.ds(8 * m, 8)] = smooth_full(lambda at, a, b: mat[at, :, a:b], c, m)
        return carry

    lax.fori_loop(0, lead // 8, smooth_z1, 0)
    pl.semaphore_wait(barrier, greeted)
    begin_lead(y1, 0, 1)

    loads[1].wait()
    loads[2].wait()
    start(*xs[0])
    row_at = lax.broadcasted_iota(jnp.int32, (rows, cols), 0)
    lane_128 = lax.broadcasted_iota(jnp.int32, (rows, 128), 1)

    def pack(r, i, k, field, sides):
        at = k * lead + i
        ys[r, 0, pl.ds(at, 1), :] = field[0:1, :]
        ys[r, 1, pl.ds(at, 1), :] = field[rows - 1:rows, :]
        low, high = sides
        low = jnp.where(lane_128 == at, pltpu.roll(field[:, 0:128], at, 1), low)
        high = jnp.where(lane_128 == at, pltpu.roll(field[:, cols - 128:cols], at + 1, 1), high)
        return low, high

    def pack_first(i, sides):
        sides = pack(0, i, 0, st0[0, i], sides)
        return pack(0, i, 1, st0[1, i], sides)

    blank = (jnp.zeros((rows, 128), F32), jnp.zeros((rows, 128), F32))
    sides = lax.fori_loop(0, lead, pack_first, blank, unroll=2)
    zsnd[0, 0], zsnd[0, 1] = sides
    start(*rs[0], *cs[0])

    def smooth_lead(src, low, high, c, put):
        for a in range(thin // 8):
            for b in range(cols // 128):
                part = (slice(None), slice(8 * a, 8 * a + 8), slice(128 * b, 128 * b + 128))
                x = jnp.concatenate([low[(c,) + part], src[(c,) + part], high[(c,) + part]], axis=0)
                put(part, tri_lead(x))

    def lead_then_chunks(halos, chunks, src, low, high, dst, put_own):
        for t in range(nz):
            c = order[t]
            near, legs_in, legs_out = halos[t]
            for leg_in, leg_out in zip(legs_in, legs_out):
                wait(leg_in)
                start(leg_out)
            if t + 2 < nz:
                finish(*legs_in, *near)
                begin_lead(halos, t + 2)
            wait(*near)
            if t < nz - 1:
                def put(part, value):
                    dst[(c,) + part] = value
                smooth_lead(src, low, high, c, put)
                start(chunks[t])
            else:
                smooth_lead(src, low, high, c, put_own)
        wait(*chunks)

    def put_tile(part, value):
        q1[:, pl.ds(pl.multiple_of(8 + thin * gz + part[1].start, 8), 8), part[2]] = value

    lead_then_chunks(y1, a1, zs, yl1, yh1, ds, put_tile)

    start(*g1)
    for k in (3, 4, 5):
        loads[k].wait()
    wait(*g1)

    def project(i, carry):
        x = tri_rows(q1[i]) * SCALE
        th = jnp.tanh(4.0 * (x - 0.5))
        dens = (TANH2 + th) * (0.5 / TANH2)
        slop = (1.0 - th * th) * (2.0 / TANH2)
        inv = 1.0 / (0.5 + dens)
        rinv[i] = 1.0 / (6.0 + 2.0 * (1.0 - dens) * inv)
        cond[i] = 1.0 - 0.8 * dens
        gain[i] = -3.0 * inv * inv * slop
        slope[i] = slop
        return carry

    lax.fori_loop(0, lead, project, 0)

    def beside(r, k, i, field):
        at = k * lead + i
        up = jnp.where(row_at == 0, yl[r, 0, pl.ds(at, 1), :], pltpu.roll(field, 1, 0))
        down = jnp.where(row_at == rows - 1, yl[r, 1, pl.ds(at, 1), :], pltpu.roll(field, rows - 1, 0))
        low = pltpu.roll(zl[r, 0], lax.rem(128 - at, 128), 1)
        high = pltpu.roll(zl[r, 1], 127 - at, 1)
        left, right = pltpu.roll(field, 1, 1), pltpu.roll(field, cols - 1, 1)
        left = jnp.concatenate([jnp.where(lane_128 == 0, low, left[:, 0:128]), left[:, 128:]], axis=1)
        right = jnp.concatenate([right[:, :cols - 128], jnp.where(lane_128 == 127, high, right[:, cols - 128:])], axis=1)
        return up, down, left, right

    def sweep(r, i, before, after):
        old, new = states[r], states[r + 1]
        s, t = old[0, i], old[1, i]
        upwind = before(1)
        marks = mark[i]
        a, b, c, d = beside(r, 0, i, s)
        total = before(0) + after(0) + ((a + b) + (c + d))
        fresh_s = (press[i] + total) * rinv[i]
        fresh_s = jnp.where(marks == 1, 1.0, jnp.where(marks == 2, 0.0, fresh_s))
        a, b, c, d = beside(r, 1, i, t)
        total = upwind + after(1) + ((a + b) + (c + d))
        h, drift = cond[i], 2.0 * s
        fresh_t = (warm[i] + h * total + drift * upwind) / (6.0 * h + drift + 0.1)
        fresh_t = jnp.where(marks == 1, 0.0, fresh_t)
        new[0, i], new[1, i] = fresh_s, fresh_t
        return fresh_s, fresh_t

    def run_sweep(r):
        old = states[r]

        def packed(i, sides, fresh):
            if r == 0:
                sides = pack(1, i, 0, fresh[0], sides)
            return pack(r + 1, i, 1, fresh[1], sides)

        def inner(i, sides):
            return packed(i, sides, sweep(r, i, lambda k: old[k, i - 1], lambda k: old[k, i + 1]))

        wait(*rs[r], *cs[r])
        if r > 0:
            sides = lax.fori_loop(1, lead - 1, inner, blank, unroll=2)
        wait(*xs[r])
        first = sweep(r, 0, lambda k: lx_lo[r, k], lambda k: old[k, 1])
        last = sweep(r, lead - 1, lambda k: old[k, lead - 2], lambda k: lx_hi[r, k])
        start(*xs[r + 1])
        if r == 0:
            sides = packed(0, blank, first)
            sides = packed(lead - 1, sides, last)
            sides = lax.fori_loop(1, lead - 1, inner, sides, unroll=2)
        else:
            sides = packed(0, sides, first)
            sides = packed(lead - 1, sides, last)
        zsnd[r + 1, 0], zsnd[r + 1, 1] = sides
        start(*rs[r + 1], *cs[r + 1])

    ys[2] = jnp.zeros(ys.shape[1:], F32)
    run_sweep(0)
    run_sweep(1)
    stores = [pltpu.make_async_copy(st2.at[0], speed_o, out_sem.at[0]), pltpu.make_async_copy(st2.at[1], temper_o, out_sem.at[1])]
    for store in stores:
        store.start()

    def spread(i, before, after):
        s, t = st2[0, i], st2[1, i]
        energy = (before - t) ** 2 + (after - t) ** 2
        for other in beside(2, 1, i, t):
            energy = energy + (other - t) ** 2
        q2[i, 8:rows + 8, :] = gain[i] * s * s - 0.4 * energy * slope[i]

    wait(*rs[2], *cs[2])

    def inner_spread(i, carry):
        spread(i, st2[1, i - 1], st2[1, i + 1])
        return carry

    lax.fori_loop(1, lead - 1, inner_spread, 0, unroll=2)
    wait(*xs[2])
    spread(0, lx_lo[2, 1], st2[1, 1])
    spread(lead - 1, st2[1, lead - 2], lx_hi[2, 1])
    start(*g2)
    wait(*g2)

    def smooth_rows(i, carry):
        x = tri_rows(q2[i])
        for c in range(nz):
            us[c, i] = x[c * thin:(c + 1) * thin, :]
        return carry

    lax.fori_loop(0, lead, smooth_rows, 0)
    begin_lead(y2, 0, 1)

    def put_slab(part, value):
        slab[(gz,) + part] = value

    lead_then_chunks(y2, a2, us, yl2, yh2, ws, put_slab)

    def columns(at, first, last):
        parts = []
        for c in range(nz):
            a, b = max(first, c * cols), min(last, (c + 1) * cols)
            if a < b:
                parts.append(slab[c, at, :, a - c * cols:b - c * cols])
        return jnp.concatenate(parts, axis=2)

    def smooth_z2(m, carry):
        for c in range(nz):
            outs[pl.ds(8 * m, 8), :, c * cols:(c + 1) * cols] = smooth_full(columns, c, m) * SCALE
        return carry

    lax.fori_loop(0, lead // 8, smooth_z2, 0)
    stores.append(pltpu.make_async_copy(outs, deriv_o, out_sem.at[2]))
    stores[2].start()

    for copy in started:
        copy.finish()
    for store in stores:
        store.wait()


def solution(mesh):
    nz = mesh.shape["gz"]

    def body(mat, mark, press, warm, vel, temp):
        lead, rows, cols = vel.shape
        thin, full = mat.shape[1:]
        tile, flat = (lead, rows, cols), (lead, thin, full)
        dma = pltpu.SemaphoreType.DMA
        vmem = lambda *shape: pltpu.VMEM(shape, F32)
        chunks, half = (nz, lead, thin, cols), (nz, 8, thin, cols)
        return pl.pallas_call(
            kernel,
            name="design_iteration",
            out_shape=[jax.ShapeDtypeStruct(tile, F32), jax.ShapeDtypeStruct(tile, F32), jax.ShapeDtypeStruct(flat, F32)],
            in_specs=[pl.BlockSpec(memory_space=pl.ANY)] * 6,
            out_specs=[pl.BlockSpec(memory_space=pl.ANY)] * 3,
            scratch_shapes=[
                vmem(*flat), pltpu.VMEM(tile, jnp.int32), vmem(*tile), vmem(*tile),
                vmem(2, *tile), vmem(2, *tile), vmem(2, *tile),
                vmem(*tile), vmem(*tile), vmem(*tile), vmem(*tile), pltpu.VMEM((cols + 256, cols), jnp.bfloat16),
                vmem(*chunks), vmem(*half), vmem(*half), vmem(*chunks),
                vmem(lead, rows + 16, cols), vmem(lead, rows + 16, cols),
                vmem(*chunks), vmem(*half), vmem(*half), vmem(*chunks), vmem(*chunks), vmem(*flat),
                vmem(nz, 8, thin // 2, cols), vmem(nz, 8, thin // 2, cols),
                vmem(3, 2, rows, cols), vmem(3, 2, rows, cols),
                vmem(3, 2, 2 * lead, cols), vmem(3, 2, 2 * lead, cols),
                vmem(3, 2, rows, 128), vmem(3, 2, rows, 128),
                dma((6,)), dma((3,)), dma((2, 104)),
            ],
            compiler_params=pltpu.CompilerParams(
                collective_id=0, has_side_effects=True, vmem_limit_bytes=60 * 1024 * 1024),
        )(mat, mark, press, warm, vel, temp)

    tiles, slabs = P("gx", "gy", "gz"), P("gx", ("gy", "gz"), None)
    return jax.shard_map(body, mesh=mesh, in_specs=(slabs,) + (tiles,) * 5, out_specs=(tiles, tiles, slabs), check_vma=False)
```

```python
import functools
import math

import jax
import jax.numpy as jnp
from jax import lax
from jax.experimental import pallas as pl
from jax.experimental.pallas import tpu as pltpu
from jax.sharding import PartitionSpec as P

MESH = pl.DeviceIdType.MESH
F32 = jnp.float32

TANH2 = math.tanh(2.0)
GROUP = 4
THROUGH = 3
SCALE = 1.0 / 81.0**3


def band_rows(n):
    row = lax.broadcasted_iota(jnp.int32, (n + 256, n), 0)
    col = lax.broadcasted_iota(jnp.int32, (n + 256, n), 1)
    return jnp.maximum(9 - jnp.abs(row - 128 - col), 0).astype(F32).astype(jnp.bfloat16)


def tri_lanes(x, band):
    top = x.astype(jnp.bfloat16)
    rest = x - top.astype(F32)
    mid = rest.astype(jnp.bfloat16)
    low = (rest - mid.astype(F32)).astype(jnp.bfloat16)
    y = jnp.dot(jnp.concatenate([top, mid, low], axis=0), band, preferred_element_type=F32)
    n = x.shape[0]
    return y[:n] + (y[n:2 * n] + y[2 * n:])


def tri_rows(x):
    n = x.shape[0]
    a = x + pltpu.roll(x, 1, 0)
    a = a + pltpu.roll(a, 2, 0)
    a = a + pltpu.roll(a, 4, 0)
    a = a + pltpu.roll(x, 8, 0)
    b = a + pltpu.roll(a, 1, 0)
    b = b + pltpu.roll(b, 2, 0)
    b = b + pltpu.roll(b, 4, 0)
    b = b + pltpu.roll(a, 8, 0)
    return b[16:]


def box_lead(x):
    a = x[1:] + x[:-1]
    a = a[2:] + a[:-2]
    a = a[4:] + a[:-4]
    return a[1:] + x[: x.shape[0] - 8]


def tri_lead(x):
    return box_lead(box_lead(x))


def smooth_full(piece, c, m, thin, cols, full, band):
    first, last = max(0, c * cols - 128), min(full, (c + 1) * cols + 128)
    skip = first - (c * cols - 128)
    x = piece(pl.ds(8 * m, 8), first, last).reshape(8 * thin, last - first)
    return tri_lanes(x, band[skip:skip + last - first, :]).reshape(8, thin, cols)


def when(condition, act):
    if condition is None:
        act()
    else:
        pl.when(condition)(act)


class Copy:
    def __init__(self, src, dst, sems, target, sends=None, receives=None, here=None):
        self.src, self.dst, self.sems, self.target = src, dst, sems, target
        self.sends, self.receives, self.here = sends, receives, dst if here is None else here

    def make(self, dst):
        return pltpu.make_async_remote_copy(src_ref=self.src, dst_ref=dst, send_sem=self.sems[0], recv_sem=self.sems[1],
                                            device_id=self.target, device_id_type=MESH)

    def start(self):
        when(self.sends, lambda: self.make(self.dst).start())

    def wait(self):
        when(self.receives, lambda: self.make(self.here).wait_recv())

    def finish(self):
        when(self.sends, lambda: self.make(self.dst).wait_send())


def kernel(mat_h, mark_h, press_h, warm_h, vel_h, temp_h, speed_o, temper_o, slab_o,
           mat, mark, press, warm, st0, st1, st2, rinv, cond, gain, slope, band,
           zs, yl1, yh1, ds, q1, q2, us, yl2, yh2, ws, slab, fy1, fy2,
           lx_lo, lx_hi, ys, yl, zsnd, zl, in_sem, out_sem, link_sem):
    gx, gy, gz = lax.axis_index("gx"), lax.axis_index("gy"), lax.axis_index("gz")
    nx, ny, nz = lax.axis_size("gx"), lax.axis_size("gy"), lax.axis_size("gz")
    lead, rows, cols = st0.shape[1:]
    thin = rows // nz
    full = nz * cols

    loads = [pltpu.make_async_copy(src, dst, in_sem.at[k]) for k, (src, dst) in enumerate(
        [(mat_h, mat), (vel_h, st0.at[0]), (temp_h, st0.at[1]), (press_h, press), (warm_h, warm), (mark_h, mark)])]
    for load in loads:
        load.start()

    edge_first, edge_last = lax.rem(gx, GROUP) == 0, lax.rem(gx, GROUP) == GROUP - 1
    at_edge = jnp.logical_or(edge_first, edge_last)
    both = jnp.logical_and
    has_before, has_after = gx >= GROUP, gx < nx - GROUP
    partners = [("gx", gx - 1, gx > 0), ("gx", gx + 1, gx < nx - 1), ("gy", gy - 1, gy > 0), ("gy", gy + 1, gy < ny - 1)]
    if nx > GROUP:
        partners += [("gx", gx - GROUP, both(at_edge, has_before)), ("gx", gx + GROUP, both(at_edge, has_after)),
                     ("gx", gx + GROUP - 1, edge_first), ("gx", gx - GROUP + 1, edge_last)]
    barrier = pltpu.get_barrier_semaphore()
    greeted = jnp.int32(nz - 1)
    for axis, to, there in partners:
        def greet():
            pl.semaphore_signal(barrier, inc=1, device_id={axis: to}, device_id_type=MESH)
        pl.when(there)(greet)
        greeted = greeted + there.astype(jnp.int32)
    for hop in range(1, nz):
        pl.semaphore_signal(barrier, inc=1, device_id={"gz": lax.rem(gz + hop, nz)}, device_id_type=MESH)

    used = [0]

    def sems():
        used[0] += 1
        return link_sem.at[0, used[0] - 1], link_sem.at[1, used[0] - 1]

    started = []

    def start(*copies):
        for copy in copies:
            copy.start()
            started.append(copy)

    def wait(*copies):
        for copy in copies:
            copy.wait()

    def finish(*copies):
        for copy in copies:
            copy.finish()
            started.remove(copy)

    def begin_lead(halos):
        for near, legs_in, _ in halos:
            start(*legs_in)
        start(*halos[0][0])
        pass_on(halos, 0)
        start(*halos[1][0])

    def pass_on(halos, t):
        _, legs_in, legs_out = halos[t]
        for leg_in, leg_out in zip(legs_in, legs_out):
            wait(leg_in)
            start(leg_out)

    def exchange(axis, low, high, land_low, land_high):
        at, count = lax.axis_index(axis), lax.axis_size(axis)

        @pl.when(at == 0)
        def _():
            land_low[...] = jnp.zeros(land_low.shape, F32)

        @pl.when(at == count - 1)
        def _():
            land_high[...] = jnp.zeros(land_high.shape, F32)

        return (Copy(high, land_low, sems(), {axis: at + 1}, at < count - 1, at > 0),
                Copy(low, land_high, sems(), {axis: at - 1}, at > 0, at < count - 1))

    hops = [2, 1, 3, 0] if nz == 4 else list(range(1, nz)) + [0]
    order = [lax.rem(gz + hop, nz) for hop in hops]

    def lead_halos(src, low, high, held):
        @pl.when(gx == 0)
        def _():
            low[...] = jnp.zeros(low.shape, F32)

        @pl.when(gx == nx - 1)
        def _():
            high[...] = jnp.zeros(high.shape, F32)

        h = thin // 2
        plans = []
        for t in range(nz):
            c = order[t]
            near, legs_in, legs_out = [], [], []
            for up in (True, False):
                out = src.at[c, lead - 8:lead] if up else src.at[c, 0:8]
                land = (low if up else high).at[c]
                step = 1 if up else -1
                sends, receives = (gx < nx - 1, gx > 0) if up else (gx > 0, gx < nx - 1)
                crosses = both(edge_last, sends) if up else both(edge_first, sends)
                if nx > GROUP and t < THROUGH:
                    near.append(Copy(out.at[:, 0:h], land.at[:, 0:h], sems(), {"gx": gx + step}, sends, receives))
                    pair = sems()
                    direct = both(sends, jnp.logical_not(crosses))
                    near.append(Copy(out.at[:, h:], land.at[:, h:], pair, {"gx": gx + step}, direct, receives))
                    first, second = -step * (GROUP - 1), step * GROUP
                    holds = both(edge_first, has_after) if up else both(edge_last, has_before)
                    legs_in.append(Copy(out.at[:, h:], held.at[t], sems(), {"gx": gx + first}, crosses, holds))
                    legs_out.append(Copy(held.at[t], land.at[:, h:], (sems()[0], pair[1]), {"gx": gx + second}, holds))
                else:
                    near.append(Copy(out, land, sems(), {"gx": gx + step}, sends, receives))
            plans.append((near, legs_in, legs_out))
        return plans

    def to_chunks(src, place):
        return [Copy(src.at[order[t]], place(gz), sems(), {"gz": order[t]}, here=place(lax.rem(gz + nz - hops[t], nz)))
                for t in range(nz - 1)]

    def tile_rows(g):
        return q1.at[:, pl.ds(pl.multiple_of(8 + thin * g, 8), thin), :]

    y1, y2 = lead_halos(zs, yl1, yh1, fy1), lead_halos(us, yl2, yh2, fy2)
    a1, a2 = to_chunks(ds, tile_rows), to_chunks(ws, lambda g: slab.at[g])
    g1 = exchange("gy", q1.at[:, 8:16], q1.at[:, rows:rows + 8], q1.at[:, 0:8], q1.at[:, rows + 8:rows + 16])
    g2 = []
    for part in (slice(1, lead - 1), slice(0, 1), slice(lead - 1, lead)):
        g2.append(exchange("gy", q2.at[part, 8:16], q2.at[part, rows:rows + 8], q2.at[part, 0:8], q2.at[part, rows + 8:rows + 16]))
    states = (st0, st1, st2)
    xs, rs, cs = [], [], []
    for r in range(3):
        which = slice(1, 2) if r == 2 else slice(0, 2)
        xs.append(exchange("gx", states[r].at[which, 0], states[r].at[which, lead - 1], lx_lo.at[r, which], lx_hi.at[r, which]))
        rs.append(exchange("gy", ys.at[r, 0], ys.at[r, 1], yl.at[r, 0], yl.at[r, 1]))
        cs.append(exchange("gz", zsnd.at[r, 0], zsnd.at[r, 1], zl.at[r, 0], zl.at[r, 1]))

    band[...] = band_rows(cols)
    loads[0].wait()

    def smooth_z1(m, carry):
        for c in range(nz):
            zs[c, pl.ds(8 * m, 8)] = smooth_full(lambda at, a, b: mat[at, :, a:b], c, m, thin, cols, full, band)
        return carry

    lax.fori_loop(0, lead // 8, smooth_z1, 0)
    pl.semaphore_wait(barrier, greeted)
    begin_lead(y1)

    loads[1].wait()
    loads[2].wait()
    start(*xs[0])
    row_at = lax.broadcasted_iota(jnp.int32, (rows, cols), 0)
    lane_128 = lax.broadcasted_iota(jnp.int32, (rows, 128), 1)

    def pack(r, i, k, field, sides):
        at = k * lead + i
        ys[r, 0, pl.ds(at, 1), :] = field[0:1, :]
        ys[r, 1, pl.ds(at, 1), :] = field[rows - 1:rows, :]
        low, high = sides
        low = jnp.where(lane_128 == at, pltpu.roll(field[:, 0:128], at, 1), low)
        high = jnp.where(lane_128 == at, pltpu.roll(field[:, cols - 128:cols], at + 1, 1), high)
        return low, high

    def pack_first(i, sides):
        sides = pack(0, i, 0, st0[0, i], sides)
        return pack(0, i, 1, st0[1, i], sides)

    blank = (jnp.zeros((rows, 128), F32), jnp.zeros((rows, 128), F32))
    sides = lax.fori_loop(0, lead, pack_first, blank, unroll=2)
    zsnd[0, 0], zsnd[0, 1] = sides
    start(*rs[0], *cs[0])

    def smooth_lead(src, low, high, c, put):
        for a in range(thin // 8):
            for b in range(cols // 128):
                part = (slice(None), slice(8 * a, 8 * a + 8), slice(128 * b, 128 * b + 128))
                x = jnp.concatenate([low[(c,) + part], src[(c,) + part], high[(c,) + part]], axis=0)
                put(part, tri_lead(x))

    def lead_then_chunks(halos, chunks, src, low, high, dst, put_own):
        for t in range(nz):
            c, near = order[t], halos[t][0]
            if t + 1 < nz:
                pass_on(halos, t + 1)
            if t + 2 < nz:
                finish(*near)
                start(*halos[t + 2][0])
            wait(*near)
            if t < nz - 1:
                def put(part, value):
                    dst[(c,) + part] = value
                smooth_lead(src, low, high, c, put)
                start(chunks[t])
            else:
                smooth_lead(src, low, high, c, put_own)
        wait(*chunks)

    def put_tile(part, value):
        q1[:, pl.ds(pl.multiple_of(8 + thin * gz + part[1].start, 8), 8), part[2]] = value

    lead_then_chunks(y1, a1, zs, yl1, yh1, ds, put_tile)

    start(*g1)
    for k in (3, 4, 5):
        loads[k].wait()
    wait(*g1)

    def project(i, carry):
        x = tri_rows(q1[i]) * SCALE
        th = jnp.tanh(4.0 * (x - 0.5))
        dens = (TANH2 + th) * (0.5 / TANH2)
        slop = (1.0 - th * th) * (2.0 / TANH2)
        inv = 1.0 / (0.5 + dens)
        rinv[i] = 1.0 / (6.0 + 2.0 * (1.0 - dens) * inv)
        cond[i] = 1.0 - 0.8 * dens
        gain[i] = -3.0 * inv * inv * slop
        slope[i] = slop
        return carry

    lax.fori_loop(0, lead, project, 0)

    def beside(r, k, i, field):
        at = k * lead + i
        up = jnp.where(row_at == 0, yl[r, 0, pl.ds(at, 1), :], pltpu.roll(field, 1, 0))
        down = jnp.where(row_at == rows - 1, yl[r, 1, pl.ds(at, 1), :], pltpu.roll(field, rows - 1, 0))
        low = pltpu.roll(zl[r, 0], lax.rem(128 - at, 128), 1)
        high = pltpu.roll(zl[r, 1], 127 - at, 1)
        left, right = pltpu.roll(field, 1, 1), pltpu.roll(field, cols - 1, 1)
        left = jnp.concatenate([jnp.where(lane_128 == 0, low, left[:, 0:128]), left[:, 128:]], axis=1)
        right = jnp.concatenate([right[:, :cols - 128], jnp.where(lane_128 == 127, high, right[:, cols - 128:])], axis=1)
        return up, down, left, right

    def sweep(r, i, before, after):
        old, new = states[r], states[r + 1]
        s, t = old[0, i], old[1, i]
        upwind = before(1)
        marks = mark[i]
        a, b, c, d = beside(r, 0, i, s)
        total = before(0) + after(0) + ((a + b) + (c + d))
        fresh_s = (press[i] + total) * rinv[i]
        fresh_s = jnp.where(marks == 1, 1.0, jnp.where(marks == 2, 0.0, fresh_s))
        a, b, c, d = beside(r, 1, i, t)
        total = upwind + after(1) + ((a + b) + (c + d))
        h, drift = cond[i], 2.0 * s
        fresh_t = (warm[i] + h * total + drift * upwind) / (6.0 * h + drift + 0.1)
        fresh_t = jnp.where(marks == 1, 0.0, fresh_t)
        new[0, i], new[1, i] = fresh_s, fresh_t
        return fresh_s, fresh_t

    def run_sweep(r):
        old = states[r]

        def packed(i, sides, fresh):
            if r == 0:
                sides = pack(1, i, 0, fresh[0], sides)
            return pack(r + 1, i, 1, fresh[1], sides)

        def inner(i, sides):
            return packed(i, sides, sweep(r, i, lambda k: old[k, i - 1], lambda k: old[k, i + 1]))

        wait(*rs[r], *cs[r])
        if r > 0:
            sides = lax.fori_loop(1, lead - 1, inner, blank, unroll=2)
        wait(*xs[r])
        first = sweep(r, 0, lambda k: lx_lo[r, k], lambda k: old[k, 1])
        last = sweep(r, lead - 1, lambda k: old[k, lead - 2], lambda k: lx_hi[r, k])
        start(*xs[r + 1])
        if r == 0:
            sides = packed(0, blank, first)
            sides = packed(lead - 1, sides, last)
            sides = lax.fori_loop(1, lead - 1, inner, sides, unroll=2)
        else:
            sides = packed(0, sides, first)
            sides = packed(lead - 1, sides, last)
        zsnd[r + 1, 0], zsnd[r + 1, 1] = sides
        start(*rs[r + 1], *cs[r + 1])

    ys[2] = jnp.zeros(ys.shape[1:], F32)
    run_sweep(0)
    run_sweep(1)
    stores = [pltpu.make_async_copy(st2.at[0], speed_o, out_sem.at[0]), pltpu.make_async_copy(st2.at[1], temper_o, out_sem.at[1])]
    for store in stores:
        store.start()

    def spread(i, before, after):
        s, t = st2[0, i], st2[1, i]
        energy = (before - t) ** 2 + (after - t) ** 2
        for other in beside(2, 1, i, t):
            energy = energy + (other - t) ** 2
        q2[i, 8:rows + 8, :] = gain[i] * s * s - 0.4 * energy * slope[i]

    wait(*rs[2], *cs[2])

    def inner_spread(i, carry):
        spread(i, st2[1, i - 1], st2[1, i + 1])
        return carry

    lax.fori_loop(1, lead - 1, inner_spread, 0, unroll=2)
    start(*g2[0])
    wait(*xs[2])
    spread(0, lx_lo[2, 1], st2[1, 1])
    spread(lead - 1, st2[1, lead - 2], lx_hi[2, 1])
    start(*g2[1], *g2[2])
    wait(*g2[0])

    def smooth_rows(i, carry):
        x = tri_rows(q2[i])
        for c in range(nz):
            us[c, i] = x[c * thin:(c + 1) * thin, :]
        return carry

    lax.fori_loop(1, lead - 1, smooth_rows, 0, unroll=2)
    wait(*g2[1], *g2[2])
    smooth_rows(0, 0)
    smooth_rows(lead - 1, 0)
    begin_lead(y2)

    def put_slab(part, value):
        slab[(gz,) + part] = value

    lead_then_chunks(y2, a2, us, yl2, yh2, ws, put_slab)

    stores.append(pltpu.make_async_copy(slab, slab_o, out_sem.at[2]))
    stores[2].start()

    for copy in started:
        copy.finish()
    for store in stores:
        store.wait()


def last_kernel(speed_h, temper_h, slab_h, speed_o, temper_o, deriv_o, slab, outs, band, in_sem, out_sem):
    nz, lead, thin, cols = slab.shape
    moves = [pltpu.make_async_copy(speed_h, speed_o, out_sem.at[0]), pltpu.make_async_copy(temper_h, temper_o, out_sem.at[1])]
    halves = [pl.ds(8 * m, 8) for m in range(lead // 8)]
    loads = [pltpu.make_async_copy(slab_h.at[:, at], slab.at[:, at], in_sem.at[m]) for m, at in enumerate(halves)]
    for copy in loads + moves:
        copy.start()
    band[...] = band_rows(cols)

    def columns(at, first, last):
        parts = []
        for c in range(nz):
            a, b = max(first, c * cols), min(last, (c + 1) * cols)
            if a < b:
                parts.append(slab[c, at, :, a - c * cols:b - c * cols])
        return jnp.concatenate(parts, axis=2)

    for m, at in enumerate(halves):
        loads[m].wait()
        for c in range(nz):
            outs[at, :, c * cols:(c + 1) * cols] = smooth_full(columns, c, m, thin, cols, nz * cols, band) * SCALE
        moves.append(pltpu.make_async_copy(outs.at[at], deriv_o.at[at], out_sem.at[2 + m]))
        moves[-1].start()
    for move in moves:
        move.wait()


def solution(mesh):
    nz = mesh.shape["gz"]

    def body(mat, mark, press, warm, vel, temp):
        lead, rows, cols = vel.shape
        thin, full = mat.shape[1:]
        tile, flat = (lead, rows, cols), (lead, thin, full)
        dma = pltpu.SemaphoreType.DMA
        vmem = lambda *shape: pltpu.VMEM(shape, F32)
        chunks, half = (nz, lead, thin, cols), (nz, 8, thin, cols)
        speed, temper, slab = pl.pallas_call(
            kernel,
            name="design_iteration",
            out_shape=[jax.ShapeDtypeStruct(tile, F32), jax.ShapeDtypeStruct(tile, F32), jax.ShapeDtypeStruct(chunks, F32)],
            in_specs=[pl.BlockSpec(memory_space=pl.ANY)] * 6,
            out_specs=[pl.BlockSpec(memory_space=pl.ANY)] * 3,
            scratch_shapes=[
                vmem(*flat), pltpu.VMEM(tile, jnp.int32), vmem(*tile), vmem(*tile),
                vmem(2, *tile), vmem(2, *tile), vmem(2, *tile),
                vmem(*tile), vmem(*tile), vmem(*tile), vmem(*tile), pltpu.VMEM((cols + 256, cols), jnp.bfloat16),
                vmem(*chunks), vmem(*half), vmem(*half), vmem(*chunks),
                vmem(lead, rows + 16, cols), vmem(lead, rows + 16, cols),
                vmem(*chunks), vmem(*half), vmem(*half), vmem(*chunks), vmem(*chunks),
                vmem(nz, 8, thin // 2, cols), vmem(nz, 8, thin // 2, cols),
                vmem(3, 2, rows, cols), vmem(3, 2, rows, cols),
                vmem(3, 2, 2 * lead, cols), vmem(3, 2, 2 * lead, cols),
                vmem(3, 2, rows, 128), vmem(3, 2, rows, 128),
                dma((6,)), dma((3,)), dma((2, 112)),
            ],
            compiler_params=pltpu.CompilerParams(
                collective_id=0, has_side_effects=True, vmem_limit_bytes=60 * 1024 * 1024),
        )(mat, mark, press, warm, vel, temp)
        return pl.pallas_call(
            last_kernel,
            name="last_filter",
            out_shape=[jax.ShapeDtypeStruct(tile, F32), jax.ShapeDtypeStruct(tile, F32), jax.ShapeDtypeStruct(flat, F32)],
            in_specs=[pl.BlockSpec(memory_space=pl.ANY)] * 3,
            out_specs=[pl.BlockSpec(memory_space=pl.ANY)] * 3,
            scratch_shapes=[vmem(*chunks), vmem(*flat), pltpu.VMEM((cols + 256, cols), jnp.bfloat16),
                            dma((lead // 8,)), dma((2 + lead // 8,))],
            compiler_params=pltpu.CompilerParams(vmem_limit_bytes=48 * 1024 * 1024),
        )(speed, temper, slab)

    tiles, slabs = P("gx", "gy", "gz"), P("gx", ("gy", "gz"), None)
    return jax.shard_map(body, mesh=mesh, in_specs=(slabs,) + (tiles,) * 5, out_specs=(tiles, tiles, slabs), check_vma=False)
```

```python
import functools
import math

import jax
import jax.numpy as jnp
from jax import lax
from jax.experimental import pallas as pl
from jax.experimental.pallas import tpu as pltpu
from jax.sharding import PartitionSpec as P

MESH = pl.DeviceIdType.MESH
F32 = jnp.float32

TANH2 = math.tanh(2.0)
GROUP = 4
THROUGH = 3
SCALE = 1.0 / 81.0**3


def band_rows(n):
    row = lax.broadcasted_iota(jnp.int32, (n + 256, n), 0)
    col = lax.broadcasted_iota(jnp.int32, (n + 256, n), 1)
    return jnp.maximum(9 - jnp.abs(row - 128 - col), 0).astype(F32).astype(jnp.bfloat16)


def tri_lanes(x, band):
    top = x.astype(jnp.bfloat16)
    rest = x - top.astype(F32)
    mid = rest.astype(jnp.bfloat16)
    low = (rest - mid.astype(F32)).astype(jnp.bfloat16)
    y = jnp.dot(jnp.concatenate([top, mid, low], axis=0), band, preferred_element_type=F32)
    n = x.shape[0]
    return y[:n] + (y[n:2 * n] + y[2 * n:])


def tri_rows(x):
    n = x.shape[0]
    a = x + pltpu.roll(x, 1, 0)
    a = a + pltpu.roll(a, 2, 0)
    a = a + pltpu.roll(a, 4, 0)
    a = a + pltpu.roll(x, 8, 0)
    b = a + pltpu.roll(a, 1, 0)
    b = b + pltpu.roll(b, 2, 0)
    b = b + pltpu.roll(b, 4, 0)
    b = b + pltpu.roll(a, 8, 0)
    return b[16:]


def box_lead(x):
    a = x[1:] + x[:-1]
    a = a[2:] + a[:-2]
    a = a[4:] + a[:-4]
    return a[1:] + x[: x.shape[0] - 8]


def tri_lead(x):
    return box_lead(box_lead(x))


def smooth_full(piece, c, m, thin, cols, full, band):
    first, last = max(0, c * cols - 128), min(full, (c + 1) * cols + 128)
    skip = first - (c * cols - 128)
    x = piece(pl.ds(8 * m, 8), first, last).reshape(8 * thin, last - first)
    return tri_lanes(x, band[skip:skip + last - first, :]).reshape(8, thin, cols)


def when(condition, act):
    if condition is None:
        act()
    else:
        pl.when(condition)(act)


class Copy:
    def __init__(self, src, dst, sems, target, sends=None, receives=None, here=None):
        self.src, self.dst, self.sems, self.target = src, dst, sems, target
        self.sends, self.receives, self.here = sends, receives, dst if here is None else here

    def make(self, dst):
        return pltpu.make_async_remote_copy(src_ref=self.src, dst_ref=dst, send_sem=self.sems[0], recv_sem=self.sems[1],
                                            device_id=self.target, device_id_type=MESH)

    def start(self):
        when(self.sends, lambda: self.make(self.dst).start())

    def wait(self):
        when(self.receives, lambda: self.make(self.here).wait_recv())

    def finish(self):
        when(self.sends, lambda: self.make(self.dst).wait_send())


def kernel(mat_h, mark_h, press_h, warm_h, vel_h, temp_h, speed_o, temper_o, slab_o,
           mat, mark, press, warm, st0, st1, st2, rinv, cond, gain, slope, band,
           zs, yl1, yh1, ds, q1, q2, us, yl2, yh2, ws, slab, fy1, fy2,
           lx_lo, lx_hi, ys, yl, zsnd, zl, in_sem, out_sem, link_sem):
    gx, gy, gz = lax.axis_index("gx"), lax.axis_index("gy"), lax.axis_index("gz")
    nx, ny, nz = lax.axis_size("gx"), lax.axis_size("gy"), lax.axis_size("gz")
    lead, rows, cols = st0.shape[1:]
    thin = rows // nz
    full = nz * cols

    loads = [pltpu.make_async_copy(src, dst, in_sem.at[k]) for k, (src, dst) in enumerate(
        [(mat_h, mat), (vel_h, st0.at[0]), (temp_h, st0.at[1]), (press_h, press), (warm_h, warm), (mark_h, mark)])]
    for load in loads:
        load.start()

    edge_first, edge_last = lax.rem(gx, GROUP) == 0, lax.rem(gx, GROUP) == GROUP - 1
    at_edge = jnp.logical_or(edge_first, edge_last)
    both = jnp.logical_and
    has_before, has_after = gx >= GROUP, gx < nx - GROUP
    partners = [("gx", gx - 1, gx > 0), ("gx", gx + 1, gx < nx - 1), ("gy", gy - 1, gy > 0), ("gy", gy + 1, gy < ny - 1)]
    if nx > GROUP:
        partners += [("gx", gx - GROUP, both(at_edge, has_before)), ("gx", gx + GROUP, both(at_edge, has_after)),
                     ("gx", gx + GROUP - 1, edge_first), ("gx", gx - GROUP + 1, edge_last)]
    barrier = pltpu.get_barrier_semaphore()
    greeted = jnp.int32(nz - 1)
    for axis, to, there in partners:
        def greet():
            pl.semaphore_signal(barrier, inc=1, device_id={axis: to}, device_id_type=MESH)
        pl.when(there)(greet)
        greeted = greeted + there.astype(jnp.int32)
    for hop in range(1, nz):
        pl.semaphore_signal(barrier, inc=1, device_id={"gz": lax.rem(gz + hop, nz)}, device_id_type=MESH)

    used = [0]

    def sems():
        used[0] += 1
        return link_sem.at[0, used[0] - 1], link_sem.at[1, used[0] - 1]

    started = []

    def start(*copies):
        for copy in copies:
            copy.start()
            started.append(copy)

    def wait(*copies):
        for copy in copies:
            copy.wait()

    def finish(*copies):
        for copy in copies:
            copy.finish()
            started.remove(copy)

    def begin_lead(halos):
        for near, legs_in, _ in halos:
            start(*legs_in)
        start(*halos[0][0])
        pass_on(halos, 0)
        start(*halos[1][0])

    def pass_on(halos, t):
        _, legs_in, legs_out = halos[t]
        for leg_in, leg_out in zip(legs_in, legs_out):
            wait(leg_in)
            start(leg_out)

    def exchange(axis, low, high, land_low, land_high):
        at, count = lax.axis_index(axis), lax.axis_size(axis)

        @pl.when(at == 0)
        def _():
            land_low[...] = jnp.zeros(land_low.shape, F32)

        @pl.when(at == count - 1)
        def _():
            land_high[...] = jnp.zeros(land_high.shape, F32)

        return (Copy(high, land_low, sems(), {axis: at + 1}, at < count - 1, at > 0),
                Copy(low, land_high, sems(), {axis: at - 1}, at > 0, at < count - 1))

    hops = [2, 1, 3, 0] if nz == 4 else list(range(1, nz)) + [0]
    order = [lax.rem(gz + hop, nz) for hop in hops]

    def lead_halos(src, low, high, held):
        @pl.when(gx == 0)
        def _():
            low[...] = jnp.zeros(low.shape, F32)

        @pl.when(gx == nx - 1)
        def _():
            high[...] = jnp.zeros(high.shape, F32)

        h = thin // 2
        plans = []
        for t in range(nz):
            c = order[t]
            near, legs_in, legs_out = [], [], []
            for up in (True, False):
                out = src.at[c, lead - 8:lead] if up else src.at[c, 0:8]
                land = (low if up else high).at[c]
                step = 1 if up else -1
                sends, receives = (gx < nx - 1, gx > 0) if up else (gx > 0, gx < nx - 1)
                crosses = both(edge_last, sends) if up else both(edge_first, sends)
                if nx > GROUP and t < THROUGH:
                    near.append(Copy(out.at[:, 0:h], land.at[:, 0:h], sems(), {"gx": gx + step}, sends, receives))
                    pair = sems()
                    direct = both(sends, jnp.logical_not(crosses))
                    near.append(Copy(out.at[:, h:], land.at[:, h:], pair, {"gx": gx + step}, direct, receives))
                    first, second = -step * (GROUP - 1), step * GROUP
                    holds = both(edge_first, has_after) if up else both(edge_last, has_before)
                    legs_in.append(Copy(out.at[:, h:], held.at[t], sems(), {"gx": gx + first}, crosses, holds))
                    legs_out.append(Copy(held.at[t], land.at[:, h:], (sems()[0], pair[1]), {"gx": gx + second}, holds))
                else:
                    near.append(Copy(out, land, sems(), {"gx": gx + step}, sends, receives))
            plans.append((near, legs_in, legs_out))
        return plans

    def to_chunks(src, place):
        return [Copy(src.at[order[t]], place(gz), sems(), {"gz": order[t]}, here=place(lax.rem(gz + nz - hops[t], nz)))
                for t in range(nz - 1)]

    def tile_rows(g):
        return q1.at[:, pl.ds(pl.multiple_of(8 + thin * g, 8), thin), :]

    y1, y2 = lead_halos(zs, yl1, yh1, fy1), lead_halos(us, yl2, yh2, fy2)
    a1, a2 = to_chunks(ds, tile_rows), to_chunks(ws, lambda g: slab.at[g])
    g1 = exchange("gy", q1.at[:, 8:16], q1.at[:, rows:rows + 8], q1.at[:, 0:8], q1.at[:, rows + 8:rows + 16])
    g2 = []
    for part in (slice(1, lead - 1), slice(0, 1), slice(lead - 1, lead)):
        g2.append(exchange("gy", q2.at[part, 8:16], q2.at[part, rows:rows + 8], q2.at[part, 0:8], q2.at[part, rows + 8:rows + 16]))
    states = (st0, st1, st2)
    xs, rs, cs = [], [], []
    for r in range(3):
        which = slice(1, 2) if r == 2 else slice(0, 2)
        xs.append(exchange("gx", states[r].at[which, 0], states[r].at[which, lead - 1], lx_lo.at[r, which], lx_hi.at[r, which]))
        rs.append(exchange("gy", ys.at[r, 0], ys.at[r, 1], yl.at[r, 0], yl.at[r, 1]))
        cs.append(exchange("gz", zsnd.at[r, 0], zsnd.at[r, 1], zl.at[r, 0], zl.at[r, 1]))

    band[...] = band_rows(cols)
    loads[0].wait()

    def smooth_z1(m, carry):
        for c in range(nz):
            zs[c, pl.ds(8 * m, 8)] = smooth_full(lambda at, a, b: mat[at, :, a:b], c, m, thin, cols, full, band)
        return carry

    lax.fori_loop(0, lead // 8, smooth_z1, 0)
    pl.semaphore_wait(barrier, greeted)
    begin_lead(y1)

    loads[1].wait()
    loads[2].wait()
    row_at = lax.broadcasted_iota(jnp.int32, (rows, cols), 0)
    lane_128 = lax.broadcasted_iota(jnp.int32, (rows, 128), 1)

    def pack(r, i, k, field, sides):
        at = k * lead + i
        ys[r, 0, pl.ds(at, 1), :] = field[0:1, :]
        ys[r, 1, pl.ds(at, 1), :] = field[rows - 1:rows, :]
        low, high = sides
        low = jnp.where(lane_128 == at, pltpu.roll(field[:, 0:128], at, 1), low)
        high = jnp.where(lane_128 == at, pltpu.roll(field[:, cols - 128:cols], at + 1, 1), high)
        return low, high

    def pack_first(i, sides):
        sides = pack(0, i, 0, st0[0, i], sides)
        return pack(0, i, 1, st0[1, i], sides)

    blank = (jnp.zeros((rows, 128), F32), jnp.zeros((rows, 128), F32))
    sides = lax.fori_loop(0, lead, pack_first, blank, unroll=2)
    zsnd[0, 0], zsnd[0, 1] = sides
    start(*rs[0], *cs[0])

    def smooth_lead(src, low, high, c, put):
        for a in range(thin // 8):
            for b in range(cols // 128):
                part = (slice(None), slice(8 * a, 8 * a + 8), slice(128 * b, 128 * b + 128))
                x = jnp.concatenate([low[(c,) + part], src[(c,) + part], high[(c,) + part]], axis=0)
                put(part, tri_lead(x))

    def lead_then_chunks(halos, chunks, src, low, high, dst, put_own, late=()):
        for t in range(nz):
            c, near = order[t], halos[t][0]
            if t + 1 < nz:
                pass_on(halos, t + 1)
            if t + 2 < nz:
                finish(*near)
                start(*halos[t + 2][0])
            if t == max(nz - 3, 0):
                start(*late)
            wait(*near)
            if t < nz - 1:
                def put(part, value):
                    dst[(c,) + part] = value
                smooth_lead(src, low, high, c, put)
                start(chunks[t])
            else:
                smooth_lead(src, low, high, c, put_own)
        wait(*chunks)

    def put_tile(part, value):
        q1[:, pl.ds(pl.multiple_of(8 + thin * gz + part[1].start, 8), 8), part[2]] = value

    lead_then_chunks(y1, a1, zs, yl1, yh1, ds, put_tile, xs[0])

    start(*g1)
    for k in (3, 4, 5):
        loads[k].wait()
    wait(*g1)

    def project(i, carry):
        x = tri_rows(q1[i]) * SCALE
        th = jnp.tanh(4.0 * (x - 0.5))
        dens = (TANH2 + th) * (0.5 / TANH2)
        slop = (1.0 - th * th) * (2.0 / TANH2)
        inv = 1.0 / (0.5 + dens)
        rinv[i] = 1.0 / (6.0 + 2.0 * (1.0 - dens) * inv)
        cond[i] = 1.0 - 0.8 * dens
        gain[i] = -3.0 * inv * inv * slop
        slope[i] = slop
        return carry

    lax.fori_loop(0, lead, project, 0)

    def beside(r, k, i, field):
        at = k * lead + i
        up = jnp.where(row_at == 0, yl[r, 0, pl.ds(at, 1), :], pltpu.roll(field, 1, 0))
        down = jnp.where(row_at == rows - 1, yl[r, 1, pl.ds(at, 1), :], pltpu.roll(field, rows - 1, 0))
        low = pltpu.roll(zl[r, 0], lax.rem(128 - at, 128), 1)
        high = pltpu.roll(zl[r, 1], 127 - at, 1)
        left, right = pltpu.roll(field, 1, 1), pltpu.roll(field, cols - 1, 1)
        left = jnp.concatenate([jnp.where(lane_128 == 0, low, left[:, 0:128]), left[:, 128:]], axis=1)
        right = jnp.concatenate([right[:, :cols - 128], jnp.where(lane_128 == 127, high, right[:, cols - 128:])], axis=1)
        return up, down, left, right

    def sweep(r, i, before, after):
        old, new = states[r], states[r + 1]
        s, t = old[0, i], old[1, i]
        upwind = before(1)
        marks = mark[i]
        a, b, c, d = beside(r, 0, i, s)
        total = before(0) + after(0) + ((a + b) + (c + d))
        fresh_s = (press[i] + total) * rinv[i]
        fresh_s = jnp.where(marks == 1, 1.0, jnp.where(marks == 2, 0.0, fresh_s))
        a, b, c, d = beside(r, 1, i, t)
        total = upwind + after(1) + ((a + b) + (c + d))
        h, drift = cond[i], 2.0 * s
        fresh_t = (warm[i] + h * total + drift * upwind) / (6.0 * h + drift + 0.1)
        fresh_t = jnp.where(marks == 1, 0.0, fresh_t)
        new[0, i], new[1, i] = fresh_s, fresh_t
        return fresh_s, fresh_t

    def run_sweep(r):
        old = states[r]

        def packed(i, sides, fresh):
            if r == 0:
                sides = pack(1, i, 0, fresh[0], sides)
            return pack(r + 1, i, 1, fresh[1], sides)

        def inner(i, sides):
            return packed(i, sides, sweep(r, i, lambda k: old[k, i - 1], lambda k: old[k, i + 1]))

        wait(*rs[r], *cs[r])
        if r > 0:
            sides = lax.fori_loop(1, lead - 1, inner, blank, unroll=2)
        wait(*xs[r])
        first = sweep(r, 0, lambda k: lx_lo[r, k], lambda k: old[k, 1])
        last = sweep(r, lead - 1, lambda k: old[k, lead - 2], lambda k: lx_hi[r, k])
        start(*xs[r + 1])
        if r == 0:
            sides = packed(0, blank, first)
            sides = packed(lead - 1, sides, last)
            sides = lax.fori_loop(1, lead - 1, inner, sides, unroll=2)
        else:
            sides = packed(0, sides, first)
            sides = packed(lead - 1, sides, last)
        zsnd[r + 1, 0], zsnd[r + 1, 1] = sides
        start(*rs[r + 1], *cs[r + 1])

    ys[2] = jnp.zeros(ys.shape[1:], F32)
    run_sweep(0)
    run_sweep(1)
    stores = [pltpu.make_async_copy(st2.at[0], speed_o, out_sem.at[0]), pltpu.make_async_copy(st2.at[1], temper_o, out_sem.at[1])]
    for store in stores:
        store.start()

    def spread(i, before, after):
        s, t = st2[0, i], st2[1, i]
        energy = (before - t) ** 2 + (after - t) ** 2
        for other in beside(2, 1, i, t):
            energy = energy + (other - t) ** 2
        q2[i, 8:rows + 8, :] = gain[i] * s * s - 0.4 * energy * slope[i]

    wait(*rs[2], *cs[2])

    def inner_spread(i, carry):
        spread(i, st2[1, i - 1], st2[1, i + 1])
        return carry

    lax.fori_loop(1, lead - 1, inner_spread, 0, unroll=2)
    start(*g2[0])
    wait(*xs[2])
    spread(0, lx_lo[2, 1], st2[1, 1])
    spread(lead - 1, st2[1, lead - 2], lx_hi[2, 1])
    start(*g2[1], *g2[2])
    wait(*g2[0])

    def smooth_rows(i, carry):
        x = tri_rows(q2[i])
        for c in range(nz):
            us[c, i] = x[c * thin:(c + 1) * thin, :]
        return carry

    lax.fori_loop(1, lead - 1, smooth_rows, 0, unroll=2)
    wait(*g2[1], *g2[2])
    smooth_rows(0, 0)
    smooth_rows(lead - 1, 0)
    begin_lead(y2)

    def put_slab(part, value):
        slab[(gz,) + part] = value

    lead_then_chunks(y2, a2, us, yl2, yh2, ws, put_slab)

    stores.append(pltpu.make_async_copy(slab, slab_o, out_sem.at[2]))
    stores[2].start()

    for copy in started:
        copy.finish()
    for store in stores:
        store.wait()


def last_kernel(speed_h, temper_h, slab_h, speed_o, temper_o, deriv_o, speed, temper, slab, outs, band, in_sem, out_sem):
    nz, lead, thin, cols = slab.shape
    halves = [pl.ds(8 * m, 8) for m in range(lead // 8)]
    loads = [pltpu.make_async_copy(slab_h.at[:, at], slab.at[:, at], in_sem.at[m]) for m, at in enumerate(halves)]
    for k, (src, dst) in enumerate([(speed_h, speed), (temper_h, temper)]):
        loads.append(pltpu.make_async_copy(src, dst, in_sem.at[lead // 8 + k]))
    for load in loads:
        load.start()
    band[...] = band_rows(cols)
    moves = []

    def columns(at, first, last):
        parts = []
        for c in range(nz):
            a, b = max(first, c * cols), min(last, (c + 1) * cols)
            if a < b:
                parts.append(slab[c, at, :, a - c * cols:b - c * cols])
        return jnp.concatenate(parts, axis=2)

    for m, at in enumerate(halves):
        loads[m].wait()
        for c in range(nz):
            outs[at, :, c * cols:(c + 1) * cols] = smooth_full(columns, c, m, thin, cols, nz * cols, band) * SCALE
        moves.append(pltpu.make_async_copy(outs.at[at], deriv_o.at[at], out_sem.at[2 + m]))
        moves[-1].start()
        if m == 0:
            for k, (src, dst) in enumerate([(speed, speed_o), (temper, temper_o)]):
                loads[lead // 8 + k].wait()
                moves.append(pltpu.make_async_copy(src, dst, out_sem.at[k]))
                moves[-1].start()
    for move in moves:
        move.wait()


def solution(mesh):
    nz = mesh.shape["gz"]

    def body(mat, mark, press, warm, vel, temp):
        lead, rows, cols = vel.shape
        thin, full = mat.shape[1:]
        tile, flat = (lead, rows, cols), (lead, thin, full)
        dma = pltpu.SemaphoreType.DMA
        vmem = lambda *shape: pltpu.VMEM(shape, F32)
        chunks, half = (nz, lead, thin, cols), (nz, 8, thin, cols)
        speed, temper, slab = pl.pallas_call(
            kernel,
            name="design_iteration",
            out_shape=[jax.ShapeDtypeStruct(tile, F32), jax.ShapeDtypeStruct(tile, F32), jax.ShapeDtypeStruct(chunks, F32)],
            in_specs=[pl.BlockSpec(memory_space=pl.ANY)] * 6,
            out_specs=[pl.BlockSpec(memory_space=pl.ANY)] * 3,
            scratch_shapes=[
                vmem(*flat), pltpu.VMEM(tile, jnp.int32), vmem(*tile), vmem(*tile),
                vmem(2, *tile), vmem(2, *tile), vmem(2, *tile),
                vmem(*tile), vmem(*tile), vmem(*tile), vmem(*tile), pltpu.VMEM((cols + 256, cols), jnp.bfloat16),
                vmem(*chunks), vmem(*half), vmem(*half), vmem(*chunks),
                vmem(lead, rows + 16, cols), vmem(lead, rows + 16, cols),
                vmem(*chunks), vmem(*half), vmem(*half), vmem(*chunks), vmem(*chunks),
                vmem(nz, 8, thin // 2, cols), vmem(nz, 8, thin // 2, cols),
                vmem(3, 2, rows, cols), vmem(3, 2, rows, cols),
                vmem(3, 2, 2 * lead, cols), vmem(3, 2, 2 * lead, cols),
                vmem(3, 2, rows, 128), vmem(3, 2, rows, 128),
                dma((6,)), dma((3,)), dma((2, 112)),
            ],
            compiler_params=pltpu.CompilerParams(
                collective_id=0, has_side_effects=True, vmem_limit_bytes=60 * 1024 * 1024),
        )(mat, mark, press, warm, vel, temp)
        return pl.pallas_call(
            last_kernel,
            name="last_filter",
            out_shape=[jax.ShapeDtypeStruct(tile, F32), jax.ShapeDtypeStruct(tile, F32), jax.ShapeDtypeStruct(flat, F32)],
            in_specs=[pl.BlockSpec(memory_space=pl.ANY)] * 3,
            out_specs=[pl.BlockSpec(memory_space=pl.ANY)] * 3,
            scratch_shapes=[vmem(*tile), vmem(*tile), vmem(*chunks), vmem(*flat), pltpu.VMEM((cols + 256, cols), jnp.bfloat16),
                            dma((2 + lead // 8,)), dma((2 + lead // 8,))],
            compiler_params=pltpu.CompilerParams(vmem_limit_bytes=62 * 1024 * 1024),
        )(speed, temper, slab)

    tiles, slabs = P("gx", "gy", "gz"), P("gx", ("gy", "gz"), None)
    return jax.shard_map(body, mesh=mesh, in_specs=(slabs,) + (tiles,) * 5, out_specs=(tiles, tiles, slabs), check_vma=False)
```

```python
import functools
import math

import jax
import jax.numpy as jnp
from jax import lax
from jax.experimental import pallas as pl
from jax.experimental.pallas import tpu as pltpu
from jax.sharding import PartitionSpec as P

MESH = pl.DeviceIdType.MESH
F32 = jnp.float32

TANH2 = math.tanh(2.0)
GROUP = 4
THROUGH = 3
SCALE = 1.0 / 81.0**3


def band_rows(n):
    row = lax.broadcasted_iota(jnp.int32, (n + 256, n), 0)
    col = lax.broadcasted_iota(jnp.int32, (n + 256, n), 1)
    return jnp.maximum(9 - jnp.abs(row - 128 - col), 0).astype(F32).astype(jnp.bfloat16)


def tri_lanes(x, band):
    top = x.astype(jnp.bfloat16)
    rest = x - top.astype(F32)
    mid = rest.astype(jnp.bfloat16)
    low = (rest - mid.astype(F32)).astype(jnp.bfloat16)
    y = jnp.dot(jnp.concatenate([top, mid, low], axis=0), band, preferred_element_type=F32)
    n = x.shape[0]
    return y[:n] + (y[n:2 * n] + y[2 * n:])


def tri_rows(x):
    n = x.shape[0]
    a = x + pltpu.roll(x, 1, 0)
    a = a + pltpu.roll(a, 2, 0)
    a = a + pltpu.roll(a, 4, 0)
    a = a + pltpu.roll(x, 8, 0)
    b = a + pltpu.roll(a, 1, 0)
    b = b + pltpu.roll(b, 2, 0)
    b = b + pltpu.roll(b, 4, 0)
    b = b + pltpu.roll(a, 8, 0)
    return b[16:]


def box_lead(x):
    a = x[1:] + x[:-1]
    a = a[2:] + a[:-2]
    a = a[4:] + a[:-4]
    return a[1:] + x[: x.shape[0] - 8]


def tri_lead(x):
    return box_lead(box_lead(x))


def smooth_full(piece, c, m, thin, cols, full, band):
    first, last = max(0, c * cols - 128), min(full, (c + 1) * cols + 128)
    skip = first - (c * cols - 128)
    x = piece(pl.ds(8 * m, 8), first, last).reshape(8 * thin, last - first)
    return tri_lanes(x, band[skip:skip + last - first, :]).reshape(8, thin, cols)


def when(condition, act):
    if condition is None:
        act()
    else:
        pl.when(condition)(act)


class Copy:
    def __init__(self, src, dst, sems, target, sends=None, receives=None, here=None):
        self.src, self.dst, self.sems, self.target = src, dst, sems, target
        self.sends, self.receives, self.here = sends, receives, dst if here is None else here

    def make(self, dst):
        return pltpu.make_async_remote_copy(src_ref=self.src, dst_ref=dst, send_sem=self.sems[0], recv_sem=self.sems[1],
                                            device_id=self.target, device_id_type=MESH)

    def start(self):
        when(self.sends, lambda: self.make(self.dst).start())

    def wait(self):
        when(self.receives, lambda: self.make(self.here).wait_recv())

    def finish(self):
        when(self.sends, lambda: self.make(self.dst).wait_send())


def kernel(mat_h, mark_h, press_h, warm_h, vel_h, temp_h, speed_o, temper_o, slab_o,
           mat, mark, press, warm, st0, st1, st2, rinv, cond, gain, slope, band,
           zs, yl1, yh1, ds, q1, q2, us, yl2, yh2, ws, slab, fy1, fy2,
           lx_lo, lx_hi, ys, yl, zsnd, zl, in_sem, out_sem, link_sem):
    gx, gy, gz = lax.axis_index("gx"), lax.axis_index("gy"), lax.axis_index("gz")
    nx, ny, nz = lax.axis_size("gx"), lax.axis_size("gy"), lax.axis_size("gz")
    lead, rows, cols = st0.shape[1:]
    thin = rows // nz
    full = nz * cols

    loads = [pltpu.make_async_copy(src, dst, in_sem.at[k]) for k, (src, dst) in enumerate(
        [(mat_h, mat), (vel_h, st0.at[0]), (temp_h, st0.at[1]), (press_h, press), (warm_h, warm), (mark_h, mark)])]
    for load in loads:
        load.start()

    edge_first, edge_last = lax.rem(gx, GROUP) == 0, lax.rem(gx, GROUP) == GROUP - 1
    at_edge = jnp.logical_or(edge_first, edge_last)
    both = jnp.logical_and
    has_before, has_after = gx >= GROUP, gx < nx - GROUP
    partners = [("gx", gx - 1, gx > 0), ("gx", gx + 1, gx < nx - 1), ("gy", gy - 1, gy > 0), ("gy", gy + 1, gy < ny - 1)]
    if nx > GROUP:
        partners += [("gx", gx - GROUP, both(at_edge, has_before)), ("gx", gx + GROUP, both(at_edge, has_after)),
                     ("gx", gx + GROUP - 1, edge_first), ("gx", gx - GROUP + 1, edge_last)]
    barrier = pltpu.get_barrier_semaphore()
    greeted = jnp.int32(nz - 1)
    for axis, to, there in partners:
        def greet():
            pl.semaphore_signal(barrier, inc=1, device_id={axis: to}, device_id_type=MESH)
        pl.when(there)(greet)
        greeted = greeted + there.astype(jnp.int32)
    for hop in range(1, nz):
        pl.semaphore_signal(barrier, inc=1, device_id={"gz": lax.rem(gz + hop, nz)}, device_id_type=MESH)

    used = [0]

    def sems():
        used[0] += 1
        return link_sem.at[0, used[0] - 1], link_sem.at[1, used[0] - 1]

    started = []

    def start(*copies):
        for copy in copies:
            copy.start()
            started.append(copy)

    def wait(*copies):
        for copy in copies:
            copy.wait()

    def finish(*copies):
        for copy in copies:
            copy.finish()
            started.remove(copy)

    def begin_lead(halos):
        for near, legs_in, _ in halos:
            start(*legs_in)
        start(*halos[0][0])
        pass_on(halos, 0)
        start(*halos[1][0])

    def pass_on(halos, t):
        _, legs_in, legs_out = halos[t]
        for leg_in, leg_out in zip(legs_in, legs_out):
            wait(leg_in)
            start(leg_out)

    def exchange(axis, low, high, land_low, land_high):
        at, count = lax.axis_index(axis), lax.axis_size(axis)

        @pl.when(at == 0)
        def _():
            land_low[...] = jnp.zeros(land_low.shape, F32)

        @pl.when(at == count - 1)
        def _():
            land_high[...] = jnp.zeros(land_high.shape, F32)

        return (Copy(high, land_low, sems(), {axis: at + 1}, at < count - 1, at > 0),
                Copy(low, land_high, sems(), {axis: at - 1}, at > 0, at < count - 1))

    hops = [2, 1, 3, 0] if nz == 4 else list(range(1, nz)) + [0]
    order = [lax.rem(gz + hop, nz) for hop in hops]

    def lead_halos(src, low, high, held):
        @pl.when(gx == 0)
        def _():
            low[...] = jnp.zeros(low.shape, F32)

        @pl.when(gx == nx - 1)
        def _():
            high[...] = jnp.zeros(high.shape, F32)

        h = thin // 2
        plans = []
        for t in range(nz):
            c = order[t]
            near, legs_in, legs_out = [], [], []
            for up in (True, False):
                out = src.at[c, lead - 8:lead] if up else src.at[c, 0:8]
                land = (low if up else high).at[c]
                step = 1 if up else -1
                sends, receives = (gx < nx - 1, gx > 0) if up else (gx > 0, gx < nx - 1)
                crosses = both(edge_last, sends) if up else both(edge_first, sends)
                if nx > GROUP and t < THROUGH:
                    near.append(Copy(out.at[:, 0:h], land.at[:, 0:h], sems(), {"gx": gx + step}, sends, receives))
                    pair = sems()
                    direct = both(sends, jnp.logical_not(crosses))
                    near.append(Copy(out.at[:, h:], land.at[:, h:], pair, {"gx": gx + step}, direct, receives))
                    first, second = -step * (GROUP - 1), step * GROUP
                    holds = both(edge_first, has_after) if up else both(edge_last, has_before)
                    legs_in.append(Copy(out.at[:, h:], held.at[t], sems(), {"gx": gx + first}, crosses, holds))
                    legs_out.append(Copy(held.at[t], land.at[:, h:], (sems()[0], pair[1]), {"gx": gx + second}, holds))
                else:
                    near.append(Copy(out, land, sems(), {"gx": gx + step}, sends, receives))
            plans.append((near, legs_in, legs_out))
        return plans

    def to_chunks(src, place):
        return [Copy(src.at[order[t]], place(gz), sems(), {"gz": order[t]}, here=place(lax.rem(gz + nz - hops[t], nz)))
                for t in range(nz - 1)]

    def tile_rows(g):
        return q1.at[:, pl.ds(pl.multiple_of(8 + thin * g, 8), thin), :]

    y1, y2 = lead_halos(zs, yl1, yh1, fy1), lead_halos(us, yl2, yh2, fy2)
    a1, a2 = to_chunks(ds, tile_rows), to_chunks(ws, lambda g: slab.at[g])
    g1 = exchange("gy", q1.at[:, 8:16], q1.at[:, rows:rows + 8], q1.at[:, 0:8], q1.at[:, rows + 8:rows + 16])
    g2 = []
    for part in (slice(1, lead - 1), slice(0, 1), slice(lead - 1, lead)):
        g2.append(exchange("gy", q2.at[part, 8:16], q2.at[part, rows:rows + 8], q2.at[part, 0:8], q2.at[part, rows + 8:rows + 16]))
    states = (st0, st1, st2)
    xs, rs, cs = [], [], []
    for r in range(3):
        which = slice(1, 2) if r == 2 else slice(0, 2)
        xs.append(exchange("gx", states[r].at[which, 0], states[r].at[which, lead - 1], lx_lo.at[r, which], lx_hi.at[r, which]))
        rs.append(exchange("gy", ys.at[r, 0], ys.at[r, 1], yl.at[r, 0], yl.at[r, 1]))
        cs.append(exchange("gz", zsnd.at[r, 0], zsnd.at[r, 1], zl.at[r, 0], zl.at[r, 1]))

    band[...] = band_rows(cols)
    loads[0].wait()

    def smooth_z1(m, carry):
        for c in range(nz):
            zs[c, pl.ds(8 * m, 8)] = smooth_full(lambda at, a, b: mat[at, :, a:b], c, m, thin, cols, full, band)
        return carry

    lax.fori_loop(0, lead // 8, smooth_z1, 0)
    pl.semaphore_wait(barrier, greeted)
    begin_lead(y1)

    loads[1].wait()
    loads[2].wait()
    row_at = lax.broadcasted_iota(jnp.int32, (rows, cols), 0)
    lane_128 = lax.broadcasted_iota(jnp.int32, (rows, 128), 1)

    def pack(r, i, k, field, sides):
        at = k * lead + i
        ys[r, 0, pl.ds(at, 1), :] = field[0:1, :]
        ys[r, 1, pl.ds(at, 1), :] = field[rows - 1:rows, :]
        low, high = sides
        low = jnp.where(lane_128 == at, pltpu.roll(field[:, 0:128], at, 1), low)
        high = jnp.where(lane_128 == at, pltpu.roll(field[:, cols - 128:cols], at + 1, 1), high)
        return low, high

    def pack_first(i, sides):
        sides = pack(0, i, 0, st0[0, i], sides)
        return pack(0, i, 1, st0[1, i], sides)

    blank = (jnp.zeros((rows, 128), F32), jnp.zeros((rows, 128), F32))
    sides = lax.fori_loop(0, lead, pack_first, blank, unroll=2)
    zsnd[0, 0], zsnd[0, 1] = sides
    start(*rs[0], *cs[0])

    def smooth_lead(src, low, high, c, put):
        for a in range(thin // 8):
            for b in range(cols // 128):
                part = (slice(None), slice(8 * a, 8 * a + 8), slice(128 * b, 128 * b + 128))
                x = jnp.concatenate([low[(c,) + part], src[(c,) + part], high[(c,) + part]], axis=0)
                put(part, tri_lead(x))

    def lead_then_chunks(halos, chunks, src, low, high, dst, put_own, late=(), landed=None):
        for t in range(nz):
            c, near = order[t], halos[t][0]
            if t + 1 < nz:
                pass_on(halos, t + 1)
            if t + 2 < nz:
                finish(*near)
                start(*halos[t + 2][0])
            if t == max(nz - 3, 0):
                start(*late)
            wait(*near)
            if t < nz - 1:
                def put(part, value):
                    dst[(c,) + part] = value
                smooth_lead(src, low, high, c, put)
                start(chunks[t])
            else:
                smooth_lead(src, low, high, c, put_own)
                if landed is not None:
                    landed(c)
        for t in range(nz - 1):
            wait(chunks[t])
            if landed is not None:
                landed(lax.rem(gz + nz - hops[t], nz))

    def put_tile(part, value):
        q1[:, pl.ds(pl.multiple_of(8 + thin * gz + part[1].start, 8), 8), part[2]] = value

    lead_then_chunks(y1, a1, zs, yl1, yh1, ds, put_tile, xs[0])

    start(*g1)
    for k in (3, 4, 5):
        loads[k].wait()
    wait(*g1)

    def project(i, carry):
        x = tri_rows(q1[i]) * SCALE
        th = jnp.tanh(4.0 * (x - 0.5))
        dens = (TANH2 + th) * (0.5 / TANH2)
        slop = (1.0 - th * th) * (2.0 / TANH2)
        inv = 1.0 / (0.5 + dens)
        rinv[i] = 1.0 / (6.0 + 2.0 * (1.0 - dens) * inv)
        cond[i] = 1.0 - 0.8 * dens
        gain[i] = -3.0 * inv * inv * slop
        slope[i] = slop
        return carry

    lax.fori_loop(0, lead, project, 0)

    def beside(r, k, i, field):
        at = k * lead + i
        up = jnp.where(row_at == 0, yl[r, 0, pl.ds(at, 1), :], pltpu.roll(field, 1, 0))
        down = jnp.where(row_at == rows - 1, yl[r, 1, pl.ds(at, 1), :], pltpu.roll(field, rows - 1, 0))
        low = pltpu.roll(zl[r, 0], lax.rem(128 - at, 128), 1)
        high = pltpu.roll(zl[r, 1], 127 - at, 1)
        left, right = pltpu.roll(field, 1, 1), pltpu.roll(field, cols - 1, 1)
        left = jnp.concatenate([jnp.where(lane_128 == 0, low, left[:, 0:128]), left[:, 128:]], axis=1)
        right = jnp.concatenate([right[:, :cols - 128], jnp.where(lane_128 == 127, high, right[:, cols - 128:])], axis=1)
        return up, down, left, right

    def sweep(r, i, before, after):
        old, new = states[r], states[r + 1]
        s, t = old[0, i], old[1, i]
        upwind = before(1)
        marks = mark[i]
        a, b, c, d = beside(r, 0, i, s)
        total = before(0) + after(0) + ((a + b) + (c + d))
        fresh_s = (press[i] + total) * rinv[i]
        fresh_s = jnp.where(marks == 1, 1.0, jnp.where(marks == 2, 0.0, fresh_s))
        a, b, c, d = beside(r, 1, i, t)
        total = upwind + after(1) + ((a + b) + (c + d))
        h, drift = cond[i], 2.0 * s
        fresh_t = (warm[i] + h * total + drift * upwind) / (6.0 * h + drift + 0.1)
        fresh_t = jnp.where(marks == 1, 0.0, fresh_t)
        new[0, i], new[1, i] = fresh_s, fresh_t
        return fresh_s, fresh_t

    def run_sweep(r):
        old = states[r]

        def packed(i, sides, fresh):
            if r == 0:
                sides = pack(1, i, 0, fresh[0], sides)
            return pack(r + 1, i, 1, fresh[1], sides)

        def inner(i, sides):
            return packed(i, sides, sweep(r, i, lambda k: old[k, i - 1], lambda k: old[k, i + 1]))

        wait(*rs[r], *cs[r])
        if r > 0:
            sides = lax.fori_loop(1, lead - 1, inner, blank, unroll=2)
        wait(*xs[r])
        first = sweep(r, 0, lambda k: lx_lo[r, k], lambda k: old[k, 1])
        last = sweep(r, lead - 1, lambda k: old[k, lead - 2], lambda k: lx_hi[r, k])
        start(*xs[r + 1])
        if r == 0:
            sides = packed(0, blank, first)
            sides = packed(lead - 1, sides, last)
            sides = lax.fori_loop(1, lead - 1, inner, sides, unroll=2)
        else:
            sides = packed(0, sides, first)
            sides = packed(lead - 1, sides, last)
        zsnd[r + 1, 0], zsnd[r + 1, 1] = sides
        start(*rs[r + 1], *cs[r + 1])

    ys[2] = jnp.zeros(ys.shape[1:], F32)
    run_sweep(0)
    run_sweep(1)
    stores = [pltpu.make_async_copy(st2.at[0], speed_o, out_sem.at[0]), pltpu.make_async_copy(st2.at[1], temper_o, out_sem.at[1])]
    for store in stores:
        store.start()

    def spread(i, before, after):
        s, t = st2[0, i], st2[1, i]
        energy = (before - t) ** 2 + (after - t) ** 2
        for other in beside(2, 1, i, t):
            energy = energy + (other - t) ** 2
        q2[i, 8:rows + 8, :] = gain[i] * s * s - 0.4 * energy * slope[i]

    wait(*rs[2], *cs[2])

    def inner_spread(i, carry):
        spread(i, st2[1, i - 1], st2[1, i + 1])
        return carry

    lax.fori_loop(1, lead - 1, inner_spread, 0, unroll=2)
    start(*g2[0])
    wait(*xs[2])
    spread(0, lx_lo[2, 1], st2[1, 1])
    spread(lead - 1, st2[1, lead - 2], lx_hi[2, 1])
    start(*g2[1], *g2[2])
    wait(*g2[0])

    def smooth_rows(i, carry):
        x = tri_rows(q2[i])
        for c in range(nz):
            us[c, i] = x[c * thin:(c + 1) * thin, :]
        return carry

    lax.fori_loop(1, lead - 1, smooth_rows, 0, unroll=2)
    wait(*g2[1], *g2[2])
    smooth_rows(0, 0)
    smooth_rows(lead - 1, 0)
    begin_lead(y2)

    def put_slab(part, value):
        slab[(gz,) + part] = value

    def store_slab(c):
        stores.append(pltpu.make_async_copy(slab.at[c], slab_o.at[c], out_sem.at[len(stores)]))
        stores[-1].start()

    lead_then_chunks(y2, a2, us, yl2, yh2, ws, put_slab, landed=store_slab)


    for copy in started:
        copy.finish()
    for store in stores:
        store.wait()


def last_kernel(speed_h, temper_h, slab_h, speed_o, temper_o, deriv_o, speed, temper, slab, outs, band, in_sem, out_sem):
    nz, lead, thin, cols = slab.shape
    halves = [pl.ds(8 * m, 8) for m in range(lead // 8)]
    loads = [pltpu.make_async_copy(slab_h.at[:, at], slab.at[:, at], in_sem.at[m]) for m, at in enumerate(halves)]
    for k, (src, dst) in enumerate([(speed_h, speed), (temper_h, temper)]):
        loads.append(pltpu.make_async_copy(src, dst, in_sem.at[lead // 8 + k]))
    for load in loads:
        load.start()
    band[...] = band_rows(cols)
    moves = []

    def columns(at, first, last):
        parts = []
        for c in range(nz):
            a, b = max(first, c * cols), min(last, (c + 1) * cols)
            if a < b:
                parts.append(slab[c, at, :, a - c * cols:b - c * cols])
        return jnp.concatenate(parts, axis=2)

    for m, at in enumerate(halves):
        loads[m].wait()
        for c in range(nz):
            outs[at, :, c * cols:(c + 1) * cols] = smooth_full(columns, c, m, thin, cols, nz * cols, band) * SCALE
        moves.append(pltpu.make_async_copy(outs.at[at], deriv_o.at[at], out_sem.at[2 + m]))
        moves[-1].start()
        if m == 0:
            for k, (src, dst) in enumerate([(speed, speed_o), (temper, temper_o)]):
                loads[lead // 8 + k].wait()
                moves.append(pltpu.make_async_copy(src, dst, out_sem.at[k]))
                moves[-1].start()
    for move in moves:
        move.wait()


def solution(mesh):
    nz = mesh.shape["gz"]

    def body(mat, mark, press, warm, vel, temp):
        lead, rows, cols = vel.shape
        thin, full = mat.shape[1:]
        tile, flat = (lead, rows, cols), (lead, thin, full)
        dma = pltpu.SemaphoreType.DMA
        vmem = lambda *shape: pltpu.VMEM(shape, F32)
        chunks, half = (nz, lead, thin, cols), (nz, 8, thin, cols)
        speed, temper, slab = pl.pallas_call(
            kernel,
            name="design_iteration",
            out_shape=[jax.ShapeDtypeStruct(tile, F32), jax.ShapeDtypeStruct(tile, F32), jax.ShapeDtypeStruct(chunks, F32)],
            in_specs=[pl.BlockSpec(memory_space=pl.ANY)] * 6,
            out_specs=[pl.BlockSpec(memory_space=pl.ANY)] * 3,
            scratch_shapes=[
                vmem(*flat), pltpu.VMEM(tile, jnp.int32), vmem(*tile), vmem(*tile),
                vmem(2, *tile), vmem(2, *tile), vmem(2, *tile),
                vmem(*tile), vmem(*tile), vmem(*tile), vmem(*tile), pltpu.VMEM((cols + 256, cols), jnp.bfloat16),
                vmem(*chunks), vmem(*half), vmem(*half), vmem(*chunks),
                vmem(lead, rows + 16, cols), vmem(lead, rows + 16, cols),
                vmem(*chunks), vmem(*half), vmem(*half), vmem(*chunks), vmem(*chunks),
                vmem(nz, 8, thin // 2, cols), vmem(nz, 8, thin // 2, cols),
                vmem(3, 2, rows, cols), vmem(3, 2, rows, cols),
                vmem(3, 2, 2 * lead, cols), vmem(3, 2, 2 * lead, cols),
                vmem(3, 2, rows, 128), vmem(3, 2, rows, 128),
                dma((6,)), dma((2 + nz,)), dma((2, 112)),
            ],
            compiler_params=pltpu.CompilerParams(
                collective_id=0, has_side_effects=True, vmem_limit_bytes=60 * 1024 * 1024),
        )(mat, mark, press, warm, vel, temp)
        return pl.pallas_call(
            last_kernel,
            name="last_filter",
            out_shape=[jax.ShapeDtypeStruct(tile, F32), jax.ShapeDtypeStruct(tile, F32), jax.ShapeDtypeStruct(flat, F32)],
            in_specs=[pl.BlockSpec(memory_space=pl.ANY)] * 3,
            out_specs=[pl.BlockSpec(memory_space=pl.ANY)] * 3,
            scratch_shapes=[vmem(*tile), vmem(*tile), vmem(*chunks), vmem(*flat), pltpu.VMEM((cols + 256, cols), jnp.bfloat16),
                            dma((2 + lead // 8,)), dma((2 + lead // 8,))],
            compiler_params=pltpu.CompilerParams(vmem_limit_bytes=62 * 1024 * 1024),
        )(speed, temper, slab)

    tiles, slabs = P("gx", "gy", "gz"), P("gx", ("gy", "gz"), None)
    return jax.shard_map(body, mesh=mesh, in_specs=(slabs,) + (tiles,) * 5, out_specs=(tiles, tiles, slabs), check_vma=False)
```

```python
import functools
import math

import jax
import jax.numpy as jnp
from jax import lax
from jax.experimental import pallas as pl
from jax.experimental.pallas import tpu as pltpu
from jax.sharding import PartitionSpec as P

MESH = pl.DeviceIdType.MESH
F32 = jnp.float32

TANH2 = math.tanh(2.0)
GROUP = 4
THROUGH = 3
SCALE = 1.0 / 81.0**3


def band_rows(n):
    row = lax.broadcasted_iota(jnp.int32, (n + 256, n), 0)
    col = lax.broadcasted_iota(jnp.int32, (n + 256, n), 1)
    return jnp.maximum(9 - jnp.abs(row - 128 - col), 0).astype(F32).astype(jnp.bfloat16)


def tri_lanes(x, band):
    top = x.astype(jnp.bfloat16)
    rest = x - top.astype(F32)
    mid = rest.astype(jnp.bfloat16)
    low = (rest - mid.astype(F32)).astype(jnp.bfloat16)
    y = jnp.dot(jnp.concatenate([top, mid, low], axis=0), band, preferred_element_type=F32)
    n = x.shape[0]
    return y[:n] + (y[n:2 * n] + y[2 * n:])


def tri_rows(x):
    n = x.shape[0]
    a = x + pltpu.roll(x, 1, 0)
    a = a + pltpu.roll(a, 2, 0)
    a = a + pltpu.roll(a, 4, 0)
    a = a + pltpu.roll(x, 8, 0)
    b = a + pltpu.roll(a, 1, 0)
    b = b + pltpu.roll(b, 2, 0)
    b = b + pltpu.roll(b, 4, 0)
    b = b + pltpu.roll(a, 8, 0)
    return b[16:]


def box_lead(x):
    a = x[1:] + x[:-1]
    a = a[2:] + a[:-2]
    a = a[4:] + a[:-4]
    return a[1:] + x[: x.shape[0] - 8]


def tri_lead(x):
    return box_lead(box_lead(x))


def smooth_full(piece, c, m, thin, cols, full, band):
    first, last = max(0, c * cols - 128), min(full, (c + 1) * cols + 128)
    skip = first - (c * cols - 128)
    x = piece(pl.ds(8 * m, 8), first, last).reshape(8 * thin, last - first)
    return tri_lanes(x, band[skip:skip + last - first, :]).reshape(8, thin, cols)


def when(condition, act):
    if condition is None:
        act()
    else:
        pl.when(condition)(act)


class Copy:
    def __init__(self, src, dst, sems, target, sends=None, receives=None, here=None):
        self.src, self.dst, self.sems, self.target = src, dst, sems, target
        self.sends, self.receives, self.here = sends, receives, dst if here is None else here

    def make(self, dst):
        return pltpu.make_async_remote_copy(src_ref=self.src, dst_ref=dst, send_sem=self.sems[0], recv_sem=self.sems[1],
                                            device_id=self.target, device_id_type=MESH)

    def start(self):
        when(self.sends, lambda: self.make(self.dst).start())

    def wait(self):
        when(self.receives, lambda: self.make(self.here).wait_recv())

    def finish(self):
        when(self.sends, lambda: self.make(self.dst).wait_send())


def kernel(mat_h, mark_h, press_h, warm_h, vel_h, temp_h, speed_o, temper_o, slab_o,
           mat, mark, press, warm, st0, st1, st2, rinv, cond, gain, slope, band,
           zs, yl1, yh1, ds, q1, q2, us, yl2, yh2, ws, slab, fy1, fy2,
           lx_lo, lx_hi, ys, yl, zsnd, zl, in_sem, out_sem, link_sem):
    gx, gy, gz = lax.axis_index("gx"), lax.axis_index("gy"), lax.axis_index("gz")
    nx, ny, nz = lax.axis_size("gx"), lax.axis_size("gy"), lax.axis_size("gz")
    lead, rows, cols = st0.shape[1:]
    thin = rows // nz
    full = nz * cols

    loads = [pltpu.make_async_copy(src, dst, in_sem.at[k]) for k, (src, dst) in enumerate(
        [(mat_h, mat), (vel_h, st0.at[0]), (temp_h, st0.at[1]), (press_h, press), (warm_h, warm), (mark_h, mark)])]
    for load in loads:
        load.start()

    edge_first, edge_last = lax.rem(gx, GROUP) == 0, lax.rem(gx, GROUP) == GROUP - 1
    at_edge = jnp.logical_or(edge_first, edge_last)
    both = jnp.logical_and
    has_before, has_after = gx >= GROUP, gx < nx - GROUP
    partners = [("gx", gx - 1, gx > 0), ("gx", gx + 1, gx < nx - 1), ("gy", gy - 1, gy > 0), ("gy", gy + 1, gy < ny - 1)]
    if nx > GROUP:
        partners += [("gx", gx - GROUP, both(at_edge, has_before)), ("gx", gx + GROUP, both(at_edge, has_after)),
                     ("gx", gx + GROUP - 1, edge_first), ("gx", gx - GROUP + 1, edge_last)]
    barrier = pltpu.get_barrier_semaphore()
    greeted = jnp.int32(nz - 1)
    for axis, to, there in partners:
        def greet():
            pl.semaphore_signal(barrier, inc=1, device_id={axis: to}, device_id_type=MESH)
        pl.when(there)(greet)
        greeted = greeted + there.astype(jnp.int32)
    for hop in range(1, nz):
        pl.semaphore_signal(barrier, inc=1, device_id={"gz": lax.rem(gz + hop, nz)}, device_id_type=MESH)

    used = [0]

    def sems():
        used[0] += 1
        return link_sem.at[0, used[0] - 1], link_sem.at[1, used[0] - 1]

    started = []

    def start(*copies):
        for copy in copies:
            copy.start()
            started.append(copy)

    def wait(*copies):
        for copy in copies:
            copy.wait()

    def finish(*copies):
        for copy in copies:
            copy.finish()
            started.remove(copy)

    def begin_lead(halos):
        for near, legs_in, _ in halos:
            start(*legs_in)
        start(*halos[0][0])
        pass_on(halos, 0)
        start(*halos[1][0])

    def pass_on(halos, t):
        _, legs_in, legs_out = halos[t]
        for leg_in, leg_out in zip(legs_in, legs_out):
            wait(leg_in)
            start(leg_out)

    def exchange(axis, low, high, land_low, land_high):
        at, count = lax.axis_index(axis), lax.axis_size(axis)

        @pl.when(at == 0)
        def _():
            land_low[...] = jnp.zeros(land_low.shape, F32)

        @pl.when(at == count - 1)
        def _():
            land_high[...] = jnp.zeros(land_high.shape, F32)

        return (Copy(high, land_low, sems(), {axis: at + 1}, at < count - 1, at > 0),
                Copy(low, land_high, sems(), {axis: at - 1}, at > 0, at < count - 1))

    odd = lax.rem(gy, 2)
    hops = [2, 1 + 2 * odd, 3 - 2 * odd, 0] if nz == 4 else list(range(1, nz)) + [0]
    order = [lax.rem(gz + hop, nz) for hop in hops]

    def lead_halos(src, low, high, held):
        @pl.when(gx == 0)
        def _():
            low[...] = jnp.zeros(low.shape, F32)

        @pl.when(gx == nx - 1)
        def _():
            high[...] = jnp.zeros(high.shape, F32)

        h = thin // 2
        plans = []
        for t in range(nz):
            c = order[t]
            near, legs_in, legs_out = [], [], []
            for up in (True, False):
                out = src.at[c, lead - 8:lead] if up else src.at[c, 0:8]
                land = (low if up else high).at[c]
                step = 1 if up else -1
                sends, receives = (gx < nx - 1, gx > 0) if up else (gx > 0, gx < nx - 1)
                crosses = both(edge_last, sends) if up else both(edge_first, sends)
                if nx > GROUP and t < THROUGH:
                    near.append(Copy(out.at[:, 0:h], land.at[:, 0:h], sems(), {"gx": gx + step}, sends, receives))
                    pair = sems()
                    direct = both(sends, jnp.logical_not(crosses))
                    near.append(Copy(out.at[:, h:], land.at[:, h:], pair, {"gx": gx + step}, direct, receives))
                    first, second = -step * (GROUP - 1), step * GROUP
                    holds = both(edge_first, has_after) if up else both(edge_last, has_before)
                    legs_in.append(Copy(out.at[:, h:], held.at[t], sems(), {"gx": gx + first}, crosses, holds))
                    legs_out.append(Copy(held.at[t], land.at[:, h:], (sems()[0], pair[1]), {"gx": gx + second}, holds))
                else:
                    near.append(Copy(out, land, sems(), {"gx": gx + step}, sends, receives))
            plans.append((near, legs_in, legs_out))
        return plans

    def to_chunks(src, place):
        return [Copy(src.at[order[t]], place(gz), sems(), {"gz": order[t]}, here=place(lax.rem(gz + nz - hops[t], nz)))
                for t in range(nz - 1)]

    def tile_rows(g):
        return q1.at[:, pl.ds(pl.multiple_of(8 + thin * g, 8), thin), :]

    y1, y2 = lead_halos(zs, yl1, yh1, fy1), lead_halos(us, yl2, yh2, fy2)
    a1, a2 = to_chunks(ds, tile_rows), to_chunks(ws, lambda g: slab.at[g])
    g1 = exchange("gy", q1.at[:, 8:16], q1.at[:, rows:rows + 8], q1.at[:, 0:8], q1.at[:, rows + 8:rows + 16])
    g2 = []
    for part in (slice(1, lead - 1), slice(0, 1), slice(lead - 1, lead)):
        g2.append(exchange("gy", q2.at[part, 8:16], q2.at[part, rows:rows + 8], q2.at[part, 0:8], q2.at[part, rows + 8:rows + 16]))
    states = (st0, st1, st2)
    xs, rs, cs = [], [], []
    for r in range(3):
        which = slice(1, 2) if r == 2 else slice(0, 2)
        xs.append(exchange("gx", states[r].at[which, 0], states[r].at[which, lead - 1], lx_lo.at[r, which], lx_hi.at[r, which]))
        rs.append(exchange("gy", ys.at[r, 0], ys.at[r, 1], yl.at[r, 0], yl.at[r, 1]))
        cs.append(exchange("gz", zsnd.at[r, 0], zsnd.at[r, 1], zl.at[r, 0], zl.at[r, 1]))

    band[...] = band_rows(cols)
    loads[0].wait()

    def smooth_z1(m, carry):
        for c in range(nz):
            zs[c, pl.ds(8 * m, 8)] = smooth_full(lambda at, a, b: mat[at, :, a:b], c, m, thin, cols, full, band)
        return carry

    lax.fori_loop(0, lead // 8, smooth_z1, 0)
    pl.semaphore_wait(barrier, greeted)
    begin_lead(y1)

    loads[1].wait()
    loads[2].wait()
    row_at = lax.broadcasted_iota(jnp.int32, (rows, cols), 0)
    lane_128 = lax.broadcasted_iota(jnp.int32, (rows, 128), 1)

    def pack(r, i, k, field, sides):
        at = k * lead + i
        ys[r, 0, pl.ds(at, 1), :] = field[0:1, :]
        ys[r, 1, pl.ds(at, 1), :] = field[rows - 1:rows, :]
        low, high = sides
        low = jnp.where(lane_128 == at, pltpu.roll(field[:, 0:128], at, 1), low)
        high = jnp.where(lane_128 == at, pltpu.roll(field[:, cols - 128:cols], at + 1, 1), high)
        return low, high

    def pack_first(i, sides):
        sides = pack(0, i, 0, st0[0, i], sides)
        return pack(0, i, 1, st0[1, i], sides)

    blank = (jnp.zeros((rows, 128), F32), jnp.zeros((rows, 128), F32))
    sides = lax.fori_loop(0, lead, pack_first, blank, unroll=2)
    zsnd[0, 0], zsnd[0, 1] = sides
    start(*rs[0], *cs[0])

    def smooth_lead(src, low, high, c, put):
        for a in range(thin // 8):
            for b in range(cols // 128):
                part = (slice(None), slice(8 * a, 8 * a + 8), slice(128 * b, 128 * b + 128))
                x = jnp.concatenate([low[(c,) + part], src[(c,) + part], high[(c,) + part]], axis=0)
                put(part, tri_lead(x))

    def lead_then_chunks(halos, chunks, src, low, high, dst, put_own, late=(), landed=None):
        for t in range(nz):
            c, near = order[t], halos[t][0]
            if t + 1 < nz:
                pass_on(halos, t + 1)
            if t + 2 < nz:
                finish(*near)
                start(*halos[t + 2][0])
            if t == max(nz - 3, 0):
                start(*late)
            wait(*near)
            if t < nz - 1:
                def put(part, value):
                    dst[(c,) + part] = value
                smooth_lead(src, low, high, c, put)
                start(chunks[t])
            else:
                smooth_lead(src, low, high, c, put_own)
                if landed is not None:
                    landed(c)
        for t in range(nz - 1):
            wait(chunks[t])
            if landed is not None:
                landed(lax.rem(gz + nz - hops[t], nz))

    def put_tile(part, value):
        q1[:, pl.ds(pl.multiple_of(8 + thin * gz + part[1].start, 8), 8), part[2]] = value

    lead_then_chunks(y1, a1, zs, yl1, yh1, ds, put_tile, xs[0])

    start(*g1)
    for k in (3, 4, 5):
        loads[k].wait()
    wait(*g1)

    def project(i, carry):
        x = tri_rows(q1[i]) * SCALE
        th = jnp.tanh(4.0 * (x - 0.5))
        dens = (TANH2 + th) * (0.5 / TANH2)
        slop = (1.0 - th * th) * (2.0 / TANH2)
        inv = 1.0 / (0.5 + dens)
        rinv[i] = 1.0 / (6.0 + 2.0 * (1.0 - dens) * inv)
        cond[i] = 1.0 - 0.8 * dens
        gain[i] = -3.0 * inv * inv * slop
        slope[i] = slop
        return carry

    lax.fori_loop(0, lead, project, 0)

    def beside(r, k, i, field):
        at = k * lead + i
        up = jnp.where(row_at == 0, yl[r, 0, pl.ds(at, 1), :], pltpu.roll(field, 1, 0))
        down = jnp.where(row_at == rows - 1, yl[r, 1, pl.ds(at, 1), :], pltpu.roll(field, rows - 1, 0))
        low = pltpu.roll(zl[r, 0], lax.rem(128 - at, 128), 1)
        high = pltpu.roll(zl[r, 1], 127 - at, 1)
        left, right = pltpu.roll(field, 1, 1), pltpu.roll(field, cols - 1, 1)
        left = jnp.concatenate([jnp.where(lane_128 == 0, low, left[:, 0:128]), left[:, 128:]], axis=1)
        right = jnp.concatenate([right[:, :cols - 128], jnp.where(lane_128 == 127, high, right[:, cols - 128:])], axis=1)
        return up, down, left, right

    def sweep(r, i, before, after):
        old, new = states[r], states[r + 1]
        s, t = old[0, i], old[1, i]
        upwind = before(1)
        marks = mark[i]
        a, b, c, d = beside(r, 0, i, s)
        total = before(0) + after(0) + ((a + b) + (c + d))
        fresh_s = (press[i] + total) * rinv[i]
        fresh_s = jnp.where(marks == 1, 1.0, jnp.where(marks == 2, 0.0, fresh_s))
        a, b, c, d = beside(r, 1, i, t)
        total = upwind + after(1) + ((a + b) + (c + d))
        h, drift = cond[i], 2.0 * s
        fresh_t = (warm[i] + h * total + drift * upwind) / (6.0 * h + drift + 0.1)
        fresh_t = jnp.where(marks == 1, 0.0, fresh_t)
        new[0, i], new[1, i] = fresh_s, fresh_t
        return fresh_s, fresh_t

    def run_sweep(r):
        old = states[r]

        def packed(i, sides, fresh):
            if r == 0:
                sides = pack(1, i, 0, fresh[0], sides)
            return pack(r + 1, i, 1, fresh[1], sides)

        def inner(i, sides):
            return packed(i, sides, sweep(r, i, lambda k: old[k, i - 1], lambda k: old[k, i + 1]))

        wait(*rs[r], *cs[r])
        if r > 0:
            sides = lax.fori_loop(1, lead - 1, inner, blank, unroll=2)
        wait(*xs[r])
        first = sweep(r, 0, lambda k: lx_lo[r, k], lambda k: old[k, 1])
        last = sweep(r, lead - 1, lambda k: old[k, lead - 2], lambda k: lx_hi[r, k])
        start(*xs[r + 1])
        if r == 0:
            sides = packed(0, blank, first)
            sides = packed(lead - 1, sides, last)
            sides = lax.fori_loop(1, lead - 1, inner, sides, unroll=2)
        else:
            sides = packed(0, sides, first)
            sides = packed(lead - 1, sides, last)
        zsnd[r + 1, 0], zsnd[r + 1, 1] = sides
        start(*rs[r + 1], *cs[r + 1])

    ys[2] = jnp.zeros(ys.shape[1:], F32)
    run_sweep(0)
    run_sweep(1)
    stores = [pltpu.make_async_copy(st2.at[0], speed_o, out_sem.at[0]), pltpu.make_async_copy(st2.at[1], temper_o, out_sem.at[1])]
    for store in stores:
        store.start()

    def spread(i, before, after):
        s, t = st2[0, i], st2[1, i]
        energy = (before - t) ** 2 + (after - t) ** 2
        for other in beside(2, 1, i, t):
            energy = energy + (other - t) ** 2
        q2[i, 8:rows + 8, :] = gain[i] * s * s - 0.4 * energy * slope[i]

    wait(*rs[2], *cs[2])

    def inner_spread(i, carry):
        spread(i, st2[1, i - 1], st2[1, i + 1])
        return carry

    lax.fori_loop(1, lead - 1, inner_spread, 0, unroll=2)
    start(*g2[0])
    wait(*xs[2])
    spread(0, lx_lo[2, 1], st2[1, 1])
    spread(lead - 1, st2[1, lead - 2], lx_hi[2, 1])
    start(*g2[1], *g2[2])
    wait(*g2[0])

    def smooth_rows(i, carry):
        x = tri_rows(q2[i])
        for c in range(nz):
            us[c, i] = x[c * thin:(c + 1) * thin, :]
        return carry

    lax.fori_loop(1, lead - 1, smooth_rows, 0, unroll=2)
    wait(*g2[1], *g2[2])
    smooth_rows(0, 0)
    smooth_rows(lead - 1, 0)
    begin_lead(y2)

    def put_slab(part, value):
        slab[(gz,) + part] = value

    def store_slab(c):
        stores.append(pltpu.make_async_copy(slab.at[c], slab_o.at[c], out_sem.at[len(stores)]))
        stores[-1].start()

    lead_then_chunks(y2, a2, us, yl2, yh2, ws, put_slab, landed=store_slab)


    for copy in started:
        copy.finish()
    for store in stores:
        store.wait()


def last_kernel(speed_h, temper_h, slab_h, speed_o, temper_o, deriv_o, speed, temper, slab, outs, band, in_sem, out_sem):
    nz, lead, thin, cols = slab.shape
    halves = [pl.ds(8 * m, 8) for m in range(lead // 8)]
    loads = [pltpu.make_async_copy(slab_h.at[:, at], slab.at[:, at], in_sem.at[m]) for m, at in enumerate(halves)]
    for k, (src, dst) in enumerate([(speed_h, speed), (temper_h, temper)]):
        loads.append(pltpu.make_async_copy(src, dst, in_sem.at[lead // 8 + k]))
    for load in loads:
        load.start()
    band[...] = band_rows(cols)
    moves = []

    def columns(at, first, last):
        parts = []
        for c in range(nz):
            a, b = max(first, c * cols), min(last, (c + 1) * cols)
            if a < b:
                parts.append(slab[c, at, :, a - c * cols:b - c * cols])
        return jnp.concatenate(parts, axis=2)

    for m, at in enumerate(halves):
        loads[m].wait()
        for c in range(nz):
            outs[at, :, c * cols:(c + 1) * cols] = smooth_full(columns, c, m, thin, cols, nz * cols, band) * SCALE
        moves.append(pltpu.make_async_copy(outs.at[at], deriv_o.at[at], out_sem.at[2 + m]))
        moves[-1].start()
        if m == 0:
            for k, (src, dst) in enumerate([(speed, speed_o), (temper, temper_o)]):
                loads[lead // 8 + k].wait()
                moves.append(pltpu.make_async_copy(src, dst, out_sem.at[k]))
                moves[-1].start()
    for move in moves:
        move.wait()


def solution(mesh):
    nz = mesh.shape["gz"]

    def body(mat, mark, press, warm, vel, temp):
        lead, rows, cols = vel.shape
        thin, full = mat.shape[1:]
        tile, flat = (lead, rows, cols), (lead, thin, full)
        dma = pltpu.SemaphoreType.DMA
        vmem = lambda *shape: pltpu.VMEM(shape, F32)
        chunks, half = (nz, lead, thin, cols), (nz, 8, thin, cols)
        speed, temper, slab = pl.pallas_call(
            kernel,
            name="design_iteration",
            out_shape=[jax.ShapeDtypeStruct(tile, F32), jax.ShapeDtypeStruct(tile, F32), jax.ShapeDtypeStruct(chunks, F32)],
            in_specs=[pl.BlockSpec(memory_space=pl.ANY)] * 6,
            out_specs=[pl.BlockSpec(memory_space=pl.ANY)] * 3,
            scratch_shapes=[
                vmem(*flat), pltpu.VMEM(tile, jnp.int32), vmem(*tile), vmem(*tile),
                vmem(2, *tile), vmem(2, *tile), vmem(2, *tile),
                vmem(*tile), vmem(*tile), vmem(*tile), vmem(*tile), pltpu.VMEM((cols + 256, cols), jnp.bfloat16),
                vmem(*chunks), vmem(*half), vmem(*half), vmem(*chunks),
                vmem(lead, rows + 16, cols), vmem(lead, rows + 16, cols),
                vmem(*chunks), vmem(*half), vmem(*half), vmem(*chunks), vmem(*chunks),
                vmem(nz, 8, thin // 2, cols), vmem(nz, 8, thin // 2, cols),
                vmem(3, 2, rows, cols), vmem(3, 2, rows, cols),
                vmem(3, 2, 2 * lead, cols), vmem(3, 2, 2 * lead, cols),
                vmem(3, 2, rows, 128), vmem(3, 2, rows, 128),
                dma((6,)), dma((2 + nz,)), dma((2, 112)),
            ],
            compiler_params=pltpu.CompilerParams(
                collective_id=0, has_side_effects=True, vmem_limit_bytes=60 * 1024 * 1024),
        )(mat, mark, press, warm, vel, temp)
        return pl.pallas_call(
            last_kernel,
            name="last_filter",
            out_shape=[jax.ShapeDtypeStruct(tile, F32), jax.ShapeDtypeStruct(tile, F32), jax.ShapeDtypeStruct(flat, F32)],
            in_specs=[pl.BlockSpec(memory_space=pl.ANY)] * 3,
            out_specs=[pl.BlockSpec(memory_space=pl.ANY)] * 3,
            scratch_shapes=[vmem(*tile), vmem(*tile), vmem(*chunks), vmem(*flat), pltpu.VMEM((cols + 256, cols), jnp.bfloat16),
                            dma((2 + lead // 8,)), dma((2 + lead // 8,))],
            compiler_params=pltpu.CompilerParams(vmem_limit_bytes=62 * 1024 * 1024),
        )(speed, temper, slab)

    tiles, slabs = P("gx", "gy", "gz"), P("gx", ("gy", "gz"), None)
    return jax.shard_map(body, mesh=mesh, in_specs=(slabs,) + (tiles,) * 5, out_specs=(tiles, tiles, slabs), check_vma=False)
```

```python
import functools
import math

import jax
import jax.numpy as jnp
from jax import lax
from jax.experimental import pallas as pl
from jax.experimental.pallas import tpu as pltpu
from jax.sharding import PartitionSpec as P

MESH = pl.DeviceIdType.MESH
F32 = jnp.float32

TANH2 = math.tanh(2.0)
GROUP = 4
THROUGH = 3
SCALE = 1.0 / 81.0**3


def band_rows(n):
    row = lax.broadcasted_iota(jnp.int32, (n + 256, n), 0)
    col = lax.broadcasted_iota(jnp.int32, (n + 256, n), 1)
    return jnp.maximum(9 - jnp.abs(row - 128 - col), 0).astype(F32).astype(jnp.bfloat16)


def tri_lanes(x, band):
    top = x.astype(jnp.bfloat16)
    rest = x - top.astype(F32)
    mid = rest.astype(jnp.bfloat16)
    low = (rest - mid.astype(F32)).astype(jnp.bfloat16)
    y = jnp.dot(jnp.concatenate([top, mid, low], axis=0), band, preferred_element_type=F32)
    n = x.shape[0]
    return y[:n] + (y[n:2 * n] + y[2 * n:])


def tri_rows(x):
    n = x.shape[0]
    a = x + pltpu.roll(x, 1, 0)
    a = a + pltpu.roll(a, 2, 0)
    a = a + pltpu.roll(a, 4, 0)
    a = a + pltpu.roll(x, 8, 0)
    b = a + pltpu.roll(a, 1, 0)
    b = b + pltpu.roll(b, 2, 0)
    b = b + pltpu.roll(b, 4, 0)
    b = b + pltpu.roll(a, 8, 0)
    return b[16:]


def box_lead(x):
    a = x[1:] + x[:-1]
    a = a[2:] + a[:-2]
    a = a[4:] + a[:-4]
    return a[1:] + x[: x.shape[0] - 8]


def tri_lead(x):
    return box_lead(box_lead(x))


def smooth_full(piece, c, m, thin, cols, full, band):
    first, last = max(0, c * cols - 128), min(full, (c + 1) * cols + 128)
    skip = first - (c * cols - 128)
    x = piece(pl.ds(8 * m, 8), first, last).reshape(8 * thin, last - first)
    return tri_lanes(x, band[skip:skip + last - first, :]).reshape(8, thin, cols)


def when(condition, act):
    if condition is None:
        act()
    else:
        pl.when(condition)(act)


class Copy:
    def __init__(self, src, dst, sems, target, sends=None, receives=None, here=None):
        self.src, self.dst, self.sems, self.target = src, dst, sems, target
        self.sends, self.receives, self.here = sends, receives, dst if here is None else here

    def make(self, dst):
        return pltpu.make_async_remote_copy(src_ref=self.src, dst_ref=dst, send_sem=self.sems[0], recv_sem=self.sems[1],
                                            device_id=self.target, device_id_type=MESH)

    def start(self):
        when(self.sends, lambda: self.make(self.dst).start())

    def wait(self):
        when(self.receives, lambda: self.make(self.here).wait_recv())

    def finish(self):
        when(self.sends, lambda: self.make(self.dst).wait_send())


def kernel(mat_h, mark_h, press_h, warm_h, vel_h, temp_h, speed_o, temper_o, slab_o,
           mat, mark, press, warm, st0, st1, st2, rinv, cond, gain, slope, band,
           zs, yl1, yh1, ds, q1, q2, us, yl2, yh2, ws, slab, fy1, fy2,
           lx_lo, lx_hi, ys, yl, zsnd, zl, in_sem, out_sem, link_sem):
    gx, gy, gz = lax.axis_index("gx"), lax.axis_index("gy"), lax.axis_index("gz")
    nx, ny, nz = lax.axis_size("gx"), lax.axis_size("gy"), lax.axis_size("gz")
    lead, rows, cols = st0.shape[1:]
    thin = rows // nz
    full = nz * cols

    loads = [pltpu.make_async_copy(src, dst, in_sem.at[k]) for k, (src, dst) in enumerate(
        [(mat_h, mat), (vel_h, st0.at[0]), (temp_h, st0.at[1]), (press_h, press), (warm_h, warm), (mark_h, mark)])]
    for load in loads:
        load.start()

    edge_first, edge_last = lax.rem(gx, GROUP) == 0, lax.rem(gx, GROUP) == GROUP - 1
    at_edge = jnp.logical_or(edge_first, edge_last)
    both = jnp.logical_and
    has_before, has_after = gx >= GROUP, gx < nx - GROUP
    partners = [("gx", gx - 1, gx > 0), ("gx", gx + 1, gx < nx - 1), ("gy", gy - 1, gy > 0), ("gy", gy + 1, gy < ny - 1)]
    if nx > GROUP:
        partners += [("gx", gx - GROUP, both(at_edge, has_before)), ("gx", gx + GROUP, both(at_edge, has_after)),
                     ("gx", gx + GROUP - 1, edge_first), ("gx", gx - GROUP + 1, edge_last)]
    barrier = pltpu.get_barrier_semaphore()
    greeted = jnp.int32(nz - 1)
    for axis, to, there in partners:
        def greet():
            pl.semaphore_signal(barrier, inc=1, device_id={axis: to}, device_id_type=MESH)
        pl.when(there)(greet)
        greeted = greeted + there.astype(jnp.int32)
    for hop in range(1, nz):
        pl.semaphore_signal(barrier, inc=1, device_id={"gz": lax.rem(gz + hop, nz)}, device_id_type=MESH)

    used = [0]

    def sems():
        used[0] += 1
        return link_sem.at[0, used[0] - 1], link_sem.at[1, used[0] - 1]

    started = []

    def start(*copies):
        for copy in copies:
            copy.start()
            started.append(copy)

    def wait(*copies):
        for copy in copies:
            copy.wait()

    def finish(*copies):
        for copy in copies:
            copy.finish()
            started.remove(copy)

    def begin_lead(halos):
        for near, legs_in, _ in halos:
            start(*legs_in)
        start(*halos[0][0])
        pass_on(halos, 0)
        start(*halos[1][0])

    def pass_on(halos, t):
        _, legs_in, legs_out = halos[t]
        for leg_in, leg_out in zip(legs_in, legs_out):
            wait(leg_in)
            start(leg_out)

    def exchange(axis, low, high, land_low, land_high):
        at, count = lax.axis_index(axis), lax.axis_size(axis)

        @pl.when(at == 0)
        def _():
            land_low[...] = jnp.zeros(land_low.shape, F32)

        @pl.when(at == count - 1)
        def _():
            land_high[...] = jnp.zeros(land_high.shape, F32)

        return (Copy(high, land_low, sems(), {axis: at + 1}, at < count - 1, at > 0),
                Copy(low, land_high, sems(), {axis: at - 1}, at > 0, at < count - 1))

    hops = [2, 1, 3, 0] if nz == 4 else list(range(1, nz)) + [0]
    order = [lax.rem(gz + hop, nz) for hop in hops]

    def lead_halos(src, low, high, held):
        @pl.when(gx == 0)
        def _():
            low[...] = jnp.zeros(low.shape, F32)

        @pl.when(gx == nx - 1)
        def _():
            high[...] = jnp.zeros(high.shape, F32)

        h = thin // 2
        plans = []
        for t in range(nz):
            c = order[t]
            near, legs_in, legs_out = [], [], []
            for up in (True, False):
                out = src.at[c, lead - 8:lead] if up else src.at[c, 0:8]
                land = (low if up else high).at[c]
                step = 1 if up else -1
                sends, receives = (gx < nx - 1, gx > 0) if up else (gx > 0, gx < nx - 1)
                crosses = both(edge_last, sends) if up else both(edge_first, sends)
                if nx > GROUP and t < THROUGH:
                    near.append(Copy(out.at[:, 0:h], land.at[:, 0:h], sems(), {"gx": gx + step}, sends, receives))
                    pair = sems()
                    direct = both(sends, jnp.logical_not(crosses))
                    near.append(Copy(out.at[:, h:], land.at[:, h:], pair, {"gx": gx + step}, direct, receives))
                    first, second = -step * (GROUP - 1), step * GROUP
                    holds = both(edge_first, has_after) if up else both(edge_last, has_before)
                    legs_in.append(Copy(out.at[:, h:], held.at[t], sems(), {"gx": gx + first}, crosses, holds))
                    legs_out.append(Copy(held.at[t], land.at[:, h:], (sems()[0], pair[1]), {"gx": gx + second}, holds))
                else:
                    near.append(Copy(out, land, sems(), {"gx": gx + step}, sends, receives))
            plans.append((near, legs_in, legs_out))
        return plans

    def to_chunks(src, place):
        return [Copy(src.at[order[t]], place(gz), sems(), {"gz": order[t]}, here=place(lax.rem(gz + nz - hops[t], nz)))
                for t in range(nz - 1)]

    def tile_rows(g):
        return q1.at[:, pl.ds(pl.multiple_of(8 + thin * g, 8), thin), :]

    y1, y2 = lead_halos(zs, yl1, yh1, fy1), lead_halos(us, yl2, yh2, fy2)
    a1, a2 = to_chunks(ds, tile_rows), to_chunks(ws, lambda g: slab.at[g])
    g1 = exchange("gy", q1.at[:, 8:16], q1.at[:, rows:rows + 8], q1.at[:, 0:8], q1.at[:, rows + 8:rows + 16])
    g2 = []
    for part in (slice(1, lead - 1), slice(0, 1), slice(lead - 1, lead)):
        g2.append(exchange("gy", q2.at[part, 8:16], q2.at[part, rows:rows + 8], q2.at[part, 0:8], q2.at[part, rows + 8:rows + 16]))
    states = (st0, st1, st2)
    xs, rs, cs = [], [], []
    for r in range(3):
        which = slice(1, 2) if r == 2 else slice(0, 2)
        xs.append(exchange("gx", states[r].at[which, 0], states[r].at[which, lead - 1], lx_lo.at[r, which], lx_hi.at[r, which]))
        rs.append(exchange("gy", ys.at[r, 0], ys.at[r, 1], yl.at[r, 0], yl.at[r, 1]))
        cs.append(exchange("gz", zsnd.at[r, 0], zsnd.at[r, 1], zl.at[r, 0], zl.at[r, 1]))

    band[...] = band_rows(cols)
    loads[0].wait()

    def smooth_z1(m, carry):
        for c in range(nz):
            zs[c, pl.ds(8 * m, 8)] = smooth_full(lambda at, a, b: mat[at, :, a:b], c, m, thin, cols, full, band)
        return carry

    lax.fori_loop(0, lead // 8, smooth_z1, 0)
    pl.semaphore_wait(barrier, greeted)
    begin_lead(y1)

    loads[1].wait()
    loads[2].wait()
    row_at = lax.broadcasted_iota(jnp.int32, (rows, cols), 0)
    lane_128 = lax.broadcasted_iota(jnp.int32, (rows, 128), 1)

    def pack(r, i, k, field, sides):
        at = k * lead + i
        ys[r, 0, pl.ds(at, 1), :] = field[0:1, :]
        ys[r, 1, pl.ds(at, 1), :] = field[rows - 1:rows, :]
        low, high = sides
        low = jnp.where(lane_128 == at, pltpu.roll(field[:, 0:128], at, 1), low)
        high = jnp.where(lane_128 == at, pltpu.roll(field[:, cols - 128:cols], at + 1, 1), high)
        return low, high

    def pack_first(i, sides):
        sides = pack(0, i, 0, st0[0, i], sides)
        return pack(0, i, 1, st0[1, i], sides)

    blank = (jnp.zeros((rows, 128), F32), jnp.zeros((rows, 128), F32))
    sides = lax.fori_loop(0, lead, pack_first, blank, unroll=4)
    zsnd[0, 0], zsnd[0, 1] = sides
    start(*rs[0], *cs[0])

    def smooth_lead(src, low, high, c, put):
        for a in range(thin // 8):
            for b in range(cols // 128):
                part = (slice(None), slice(8 * a, 8 * a + 8), slice(128 * b, 128 * b + 128))
                x = jnp.concatenate([low[(c,) + part], src[(c,) + part], high[(c,) + part]], axis=0)
                put(part, tri_lead(x))

    def lead_then_chunks(halos, chunks, src, low, high, dst, put_own, late=(), landed=None):
        for t in range(nz):
            c, near = order[t], halos[t][0]
            if t + 1 < nz:
                pass_on(halos, t + 1)
            if t + 2 < nz:
                finish(*near)
                start(*halos[t + 2][0])
            if t == max(nz - 3, 0):
                start(*late)
            wait(*near)
            if t < nz - 1:
                def put(part, value):
                    dst[(c,) + part] = value
                smooth_lead(src, low, high, c, put)
                start(chunks[t])
            else:
                smooth_lead(src, low, high, c, put_own)
                if landed is not None:
                    landed(c)
        for t in range(nz - 1):
            wait(chunks[t])
            if landed is not None:
                landed(lax.rem(gz + nz - hops[t], nz))

    def put_tile(part, value):
        q1[:, pl.ds(pl.multiple_of(8 + thin * gz + part[1].start, 8), 8), part[2]] = value

    lead_then_chunks(y1, a1, zs, yl1, yh1, ds, put_tile, xs[0])

    start(*g1)
    for k in (3, 4, 5):
        loads[k].wait()
    wait(*g1)

    def project(i, carry):
        x = tri_rows(q1[i]) * SCALE
        th = jnp.tanh(4.0 * (x - 0.5))
        dens = (TANH2 + th) * (0.5 / TANH2)
        slop = (1.0 - th * th) * (2.0 / TANH2)
        inv = 1.0 / (0.5 + dens)
        rinv[i] = 1.0 / (6.0 + 2.0 * (1.0 - dens) * inv)
        cond[i] = 1.0 - 0.8 * dens
        gain[i] = -3.0 * inv * inv * slop
        slope[i] = slop
        return carry

    lax.fori_loop(0, lead, project, 0)

    def beside(r, k, i, field):
        at = k * lead + i
        up = jnp.where(row_at == 0, yl[r, 0, pl.ds(at, 1), :], pltpu.roll(field, 1, 0))
        down = jnp.where(row_at == rows - 1, yl[r, 1, pl.ds(at, 1), :], pltpu.roll(field, rows - 1, 0))
        low = pltpu.roll(zl[r, 0], lax.rem(128 - at, 128), 1)
        high = pltpu.roll(zl[r, 1], 127 - at, 1)
        left, right = pltpu.roll(field, 1, 1), pltpu.roll(field, cols - 1, 1)
        left = jnp.concatenate([jnp.where(lane_128 == 0, low, left[:, 0:128]), left[:, 128:]], axis=1)
        right = jnp.concatenate([right[:, :cols - 128], jnp.where(lane_128 == 127, high, right[:, cols - 128:])], axis=1)
        return up, down, left, right

    def sweep(r, i, before, after):
        old, new = states[r], states[r + 1]
        s, t = old[0, i], old[1, i]
        upwind = before(1)
        marks = mark[i]
        a, b, c, d = beside(r, 0, i, s)
        total = before(0) + after(0) + ((a + b) + (c + d))
        fresh_s = (press[i] + total) * rinv[i]
        fresh_s = jnp.where(marks == 1, 1.0, jnp.where(marks == 2, 0.0, fresh_s))
        a, b, c, d = beside(r, 1, i, t)
        total = upwind + after(1) + ((a + b) + (c + d))
        h, drift = cond[i], 2.0 * s
        fresh_t = (warm[i] + h * total + drift * upwind) / (6.0 * h + drift + 0.1)
        fresh_t = jnp.where(marks == 1, 0.0, fresh_t)
        new[0, i], new[1, i] = fresh_s, fresh_t
        return fresh_s, fresh_t

    def run_sweep(r):
        old = states[r]

        def packed(i, sides, fresh):
            if r == 0:
                sides = pack(1, i, 0, fresh[0], sides)
            return pack(r + 1, i, 1, fresh[1], sides)

        def inner(i, sides):
            return packed(i, sides, sweep(r, i, lambda k: old[k, i - 1], lambda k: old[k, i + 1]))

        wait(*rs[r], *cs[r])
        if r > 0:
            sides = lax.fori_loop(1, lead - 1, inner, blank, unroll=4)
        wait(*xs[r])
        first = sweep(r, 0, lambda k: lx_lo[r, k], lambda k: old[k, 1])
        last = sweep(r, lead - 1, lambda k: old[k, lead - 2], lambda k: lx_hi[r, k])
        start(*xs[r + 1])
        if r == 0:
            sides = packed(0, blank, first)
            sides = packed(lead - 1, sides, last)
            sides = lax.fori_loop(1, lead - 1, inner, sides, unroll=4)
        else:
            sides = packed(0, sides, first)
            sides = packed(lead - 1, sides, last)
        zsnd[r + 1, 0], zsnd[r + 1, 1] = sides
        start(*rs[r + 1], *cs[r + 1])

    ys[2] = jnp.zeros(ys.shape[1:], F32)
    run_sweep(0)
    run_sweep(1)
    stores = [pltpu.make_async_copy(st2.at[0], speed_o, out_sem.at[0]), pltpu.make_async_copy(st2.at[1], temper_o, out_sem.at[1])]
    for store in stores:
        store.start()

    def spread(i, before, after):
        s, t = st2[0, i], st2[1, i]
        energy = (before - t) ** 2 + (after - t) ** 2
        for other in beside(2, 1, i, t):
            energy = energy + (other - t) ** 2
        q2[i, 8:rows + 8, :] = gain[i] * s * s - 0.4 * energy * slope[i]

    wait(*rs[2], *cs[2])

    def inner_spread(i, carry):
        spread(i, st2[1, i - 1], st2[1, i + 1])
        return carry

    lax.fori_loop(1, lead - 1, inner_spread, 0, unroll=4)
    start(*g2[0])
    wait(*xs[2])
    spread(0, lx_lo[2, 1], st2[1, 1])
    spread(lead - 1, st2[1, lead - 2], lx_hi[2, 1])
    start(*g2[1], *g2[2])
    wait(*g2[0])

    def smooth_rows(i, carry):
        x = tri_rows(q2[i])
        for c in range(nz):
            us[c, i] = x[c * thin:(c + 1) * thin, :]
        return carry

    lax.fori_loop(1, lead - 1, smooth_rows, 0, unroll=4)
    wait(*g2[1], *g2[2])
    smooth_rows(0, 0)
    smooth_rows(lead - 1, 0)
    begin_lead(y2)

    def put_slab(part, value):
        slab[(gz,) + part] = value

    def store_slab(c):
        stores.append(pltpu.make_async_copy(slab.at[c], slab_o.at[c], out_sem.at[len(stores)]))
        stores[-1].start()

    lead_then_chunks(y2, a2, us, yl2, yh2, ws, put_slab, landed=store_slab)


    for copy in started:
        copy.finish()
    for store in stores:
        store.wait()


def last_kernel(speed_h, temper_h, slab_h, speed_o, temper_o, deriv_o, speed, temper, slab, outs, band, in_sem, out_sem):
    nz, lead, thin, cols = slab.shape
    halves = [pl.ds(8 * m, 8) for m in range(lead // 8)]
    loads = [pltpu.make_async_copy(slab_h.at[:, at], slab.at[:, at], in_sem.at[m]) for m, at in enumerate(halves)]
    for k, (src, dst) in enumerate([(speed_h, speed), (temper_h, temper)]):
        loads.append(pltpu.make_async_copy(src, dst, in_sem.at[lead // 8 + k]))
    for load in loads:
        load.start()
    band[...] = band_rows(cols)
    moves = []

    def columns(at, first, last):
        parts = []
        for c in range(nz):
            a, b = max(first, c * cols), min(last, (c + 1) * cols)
            if a < b:
                parts.append(slab[c, at, :, a - c * cols:b - c * cols])
        return jnp.concatenate(parts, axis=2)

    for m, at in enumerate(halves):
        loads[m].wait()
        for c in range(nz):
            outs[at, :, c * cols:(c + 1) * cols] = smooth_full(columns, c, m, thin, cols, nz * cols, band) * SCALE
        moves.append(pltpu.make_async_copy(outs.at[at], deriv_o.at[at], out_sem.at[2 + m]))
        moves[-1].start()
        if m == 0:
            for k, (src, dst) in enumerate([(speed, speed_o), (temper, temper_o)]):
                loads[lead // 8 + k].wait()
                moves.append(pltpu.make_async_copy(src, dst, out_sem.at[k]))
                moves[-1].start()
    for move in moves:
        move.wait()


def solution(mesh):
    nz = mesh.shape["gz"]

    def body(mat, mark, press, warm, vel, temp):
        lead, rows, cols = vel.shape
        thin, full = mat.shape[1:]
        tile, flat = (lead, rows, cols), (lead, thin, full)
        dma = pltpu.SemaphoreType.DMA
        vmem = lambda *shape: pltpu.VMEM(shape, F32)
        chunks, half = (nz, lead, thin, cols), (nz, 8, thin, cols)
        speed, temper, slab = pl.pallas_call(
            kernel,
            name="design_iteration",
            out_shape=[jax.ShapeDtypeStruct(tile, F32), jax.ShapeDtypeStruct(tile, F32), jax.ShapeDtypeStruct(chunks, F32)],
            in_specs=[pl.BlockSpec(memory_space=pl.ANY)] * 6,
            out_specs=[pl.BlockSpec(memory_space=pl.ANY)] * 3,
            scratch_shapes=[
                vmem(*flat), pltpu.VMEM(tile, jnp.int32), vmem(*tile), vmem(*tile),
                vmem(2, *tile), vmem(2, *tile), vmem(2, *tile),
                vmem(*tile), vmem(*tile), vmem(*tile), vmem(*tile), pltpu.VMEM((cols + 256, cols), jnp.bfloat16),
                vmem(*chunks), vmem(*half), vmem(*half), vmem(*chunks),
                vmem(lead, rows + 16, cols), vmem(lead, rows + 16, cols),
                vmem(*chunks), vmem(*half), vmem(*half), vmem(*chunks), vmem(*chunks),
                vmem(nz, 8, thin // 2, cols), vmem(nz, 8, thin // 2, cols),
                vmem(3, 2, rows, cols), vmem(3, 2, rows, cols),
                vmem(3, 2, 2 * lead, cols), vmem(3, 2, 2 * lead, cols),
                vmem(3, 2, rows, 128), vmem(3, 2, rows, 128),
                dma((6,)), dma((2 + nz,)), dma((2, 112)),
            ],
            compiler_params=pltpu.CompilerParams(
                collective_id=0, has_side_effects=True, vmem_limit_bytes=60 * 1024 * 1024),
        )(mat, mark, press, warm, vel, temp)
        return pl.pallas_call(
            last_kernel,
            name="last_filter",
            out_shape=[jax.ShapeDtypeStruct(tile, F32), jax.ShapeDtypeStruct(tile, F32), jax.ShapeDtypeStruct(flat, F32)],
            in_specs=[pl.BlockSpec(memory_space=pl.ANY)] * 3,
            out_specs=[pl.BlockSpec(memory_space=pl.ANY)] * 3,
            scratch_shapes=[vmem(*tile), vmem(*tile), vmem(*chunks), vmem(*flat), pltpu.VMEM((cols + 256, cols), jnp.bfloat16),
                            dma((2 + lead // 8,)), dma((2 + lead // 8,))],
            compiler_params=pltpu.CompilerParams(vmem_limit_bytes=62 * 1024 * 1024),
        )(speed, temper, slab)

    tiles, slabs = P("gx", "gy", "gz"), P("gx", ("gy", "gz"), None)
    return jax.shard_map(body, mesh=mesh, in_specs=(slabs,) + (tiles,) * 5, out_specs=(tiles, tiles, slabs), check_vma=False)
```
